128 devices in a mesh: radial: 32 (over z, x, core), chan: 4 (over y).
Axes of the slice: x: 4, y: 4, z: 4, core: 2. Of those that a mesh axis runs over, the one named last changes fastest.
Arguments:
- outer_wave: float32 [2, 1200, 8192], P(None, 'chan', 'radial'), may hold values from -6 to 6
- inner_wave: float32 [2, 30720], P(None, 'radial'), may hold values from -1.5 to 1.5
- inner_ham: bfloat16 [30720, 30720], P('radial', 'chan'), may hold values from -15 to 15
- surface: bfloat16 [2, 1200, 30720], P(None, 'chan', 'radial'), may hold values from -0.046875 to 0.046875
- dipole: bfloat16 [1200, 1200], P('chan'), as said below
- ang_mom: int32 [1200], replicated, may hold values from 0 to 23
- target: int32 [1200], replicated, may hold values from 0 to 7
- couple_mask: int32 [8, 8], replicated, may hold values from 0 to 1, as said below
Outputs:
- outer_next: float32 [2, 1200, 8192], P(None, 'chan', 'radial')
- inner_next: float32 [2, 30720], P(None, 'radial')
The draws below stay inside these ranges and needn't reach their ends.
Inputs may be any that keep to these rules, and one draw needn't show every extreme that they name: dipole is symmetric. couple_mask is symmetric with ones on its diagonal.
All inputs are finite; a program needn't handle non-finite values.
Results may differ from the reference program's by a relative error of at most 0.0054.
Values may be sent and summed in bfloat16 or wider, within the bound.
A program may use at most 128 MiB of HBM per device.

```python
import jax
import jax.numpy as jnp
from jax import lax

NC = 1200
NI = 30720
NR = 8192
NT = 8
LMAX = 24
ORDER = 8


def draw_dipole(key, part):
    key = jax.random.fold_in(key, 11)
    scale = NC ** (-0.5)
    base = jax.random.normal(key, (NC, NC), jnp.float32)
    sym = (base + base.T) * (0.70710678 * scale)
    return sym.astype(jnp.bfloat16)


def draw_surface(key, part):
    key = jax.random.fold_in(key, 13)
    sign_key, size_key = jax.random.split(key)
    sign_part = jax.random.randint(sign_key, (2, NC, NI), 0, 2).astype(jnp.float32) * 2.0 - 1.0
    lowest = 0.03
    magnitude = jax.random.uniform(size_key, (2, NC, NI), jnp.float32, lowest, 0.046875)
    return (sign_part * magnitude).astype(jnp.bfloat16)


def draw_couple_mask(key, part):
    key = jax.random.fold_in(key, 12)
    bits = jax.random.randint(key, (NT, NT), 0, 2).astype(jnp.int32)
    rows = jnp.arange(NT)[:, None]
    cols = jnp.arange(NT)[None, :]
    upper = jnp.where(rows <= cols, bits, bits.T)
    return jnp.where(rows == cols, 1, upper).astype(jnp.int32)


def plant(array, key, least, largest):
    shape = array.shape
    spot = [jax.random.randint(jax.random.fold_in(key, axis), (), 0, shape[axis]) for axis in range(len(shape))]
    array = array.at[tuple(spot)].set(least)
    longest = shape.index(max(shape))
    spot[longest] = (spot[longest] + 1) % shape[longest]
    return array.at[tuple(spot)].set(largest)


def block_scale(rng, extent, cuts, least, top_value):
    factor_of, own = 1.0, jax.random.fold_in(rng, 6)
    for axis_at, parts in cuts:
        heights = jnp.exp(jax.random.uniform(jax.random.fold_in(own, axis_at), (parts,), jnp.float32, least / len(cuts), top_value / len(cuts)))
        factor_of = factor_of * jnp.repeat(heights, extent[axis_at] // parts).reshape([-1 if axis == axis_at else 1 for axis in range(len(extent))])
    return factor_of


def normal_values(key, shape, deviation, limit, pieces=(), dtype=jnp.bfloat16):
    factor_of = block_scale(key, shape, pieces, -0.22, 0.18) if pieces else 1.0
    values = jax.random.normal(key, shape, jnp.float32) * deviation * factor_of
    return jnp.minimum(jnp.maximum(values, -limit), limit).astype(dtype)


def setup_inputs(seed: int = 0) -> dict:
    arg_keys = jax.random.split(jax.random.key(seed), 9)
    outer_wave = normal_values(arg_keys[0], (2, NC, NR), 1.0, 6.0, ((1, 4), (2, 32)), jnp.float32)
    inner_wave = normal_values(arg_keys[1], (2, NI), 0.25, 1.5, ((1, 32),), jnp.float32)
    inner_ham = normal_values(arg_keys[2], (NI, NI), 2.5, 15.0, ((0, 32), (1, 4)))
    surface = draw_surface(jax.random.fold_in(arg_keys[8], 71), 0)
    dipole = draw_dipole(jax.random.fold_in(arg_keys[8], 71), 0)
    ang_mom = plant(jax.random.randint(arg_keys[5], (NC,), 0, LMAX), jax.random.fold_in(arg_keys[5], 1), 0, LMAX - 1).astype(jnp.int32)
    target = plant(jax.random.randint(arg_keys[6], (NC,), 0, NT), jax.random.fold_in(arg_keys[6], 1), 0, NT - 1).astype(jnp.int32)
    couple_mask = draw_couple_mask(jax.random.fold_in(arg_keys[8], 71), 0)
    return dict(outer_wave=outer_wave, inner_wave=inner_wave, inner_ham=inner_ham, surface=surface, dipole=dipole, ang_mom=ang_mom, target=target, couple_mask=couple_mask)


time_step = 0.008
grid_step = 0.08
inner_radius = 20.0
surface_gain = 16.0 / (24.0 * grid_step * grid_step)


def inner_product(inner_ham, v_half):
    blocks = inner_ham.reshape(NI // 512, 512, NI)
    vector = v_half.astype(jnp.float32)

    def one_block(rows):
        return jnp.einsum('ij,sj->si', rows.astype(jnp.float32), vector, precision=lax.Precision.HIGHEST)

    result = lax.map(one_block, blocks)
    return jnp.transpose(result, (1, 0, 2)).reshape(2, NI)


def reference(outer_wave, inner_wave, inner_ham, surface, dipole, ang_mom, target, couple_mask):
    levels = couple_mask[target][:, target]
    step_l = jnp.abs(ang_mom[:, None] - ang_mom[None, :]) == 1
    coupling = jnp.where(step_l & (levels == 1), dipole, jnp.zeros_like(dipole))
    coupling32 = coupling.astype(jnp.float32)
    surface32 = surface.astype(jnp.float32)
    radius = inner_radius + grid_step * (jnp.arange(NR).astype(jnp.float32) + 1.0)
    lvals = ang_mom.astype(jnp.float32)
    centri = (lvals * (lvals + 1.0) / 2.0)[:, None] / (radius * radius)[None, :]
    outer_term, inner_term = outer_wave, inner_wave
    outer_total, inner_total = outer_wave, inner_wave
    for order in range(1, ORDER + 1):
        u_half = outer_term.astype(jnp.bfloat16)
        v_half = inner_term.astype(jnp.bfloat16)
        ghost = jnp.einsum('mci,si->msc', surface32, v_half.astype(jnp.float32), precision=lax.Precision.HIGHEST)
        rim = jnp.stack([ghost[1], ghost[0]], axis=-1)
        padded = jnp.concatenate([rim, outer_term, jnp.zeros((2, NC, 2), jnp.float32)], axis=-1)
        lap = (-padded[..., 0:NR] + 16.0 * padded[..., 1:NR + 1] - 30.0 * padded[..., 2:NR + 2]
               + 16.0 * padded[..., 3:NR + 3] - padded[..., 4:NR + 4]) / (12.0 * grid_step * grid_step)
        mixed = jnp.einsum('ab,sbj->saj', coupling32, u_half.astype(jnp.float32), precision=lax.Precision.HIGHEST)
        outer_apply = -0.5 * lap + centri * outer_term + radius * mixed
        edge = u_half[:, :, 0:2].astype(jnp.float32)
        inner_apply = inner_product(inner_ham, v_half) + surface_gain * jnp.einsum(
            'mci,scm->si', surface32, edge, precision=lax.Precision.HIGHEST)
        factor = time_step / order
        outer_term = jnp.stack([factor * outer_apply[1], -factor * outer_apply[0]])
        inner_term = jnp.stack([factor * inner_apply[1], -factor * inner_apply[0]])
        outer_total = outer_total + outer_term
        inner_total = inner_total + inner_term
    return outer_total, inner_total
```

```python
import jax
import jax.numpy as jnp
from jax import lax
from jax.experimental import pallas as pl
from jax.experimental.pallas import tpu as pltpu
from jax.sharding import PartitionSpec as P

ORDER = 8
time_step = 0.008
grid_step = 0.08
inner_radius = 20.0
surface_gain = 16.0 / (24.0 * grid_step * grid_step)
lap_gain = 1.0 / (24.0 * grid_step * grid_step)

MESH = pl.DeviceIdType.MESH
F32, BF16 = jnp.float32, jnp.bfloat16
NRAD, NCH = 32, 4
ROWS, LC, PTS = 960, 300, 256
RP, CP = 1024, 384
SLOTS = 4
HALO, BLK = 16, 64
CR = 320
STRIP = 32
NT = (((1,), (1,)), ((), ()))


def nt_dot(a, b):
    return lax.dot_general(a, b, NT, preferred_element_type=F32)


def nn_dot(a, b):
    return jnp.dot(a, b, preferred_element_type=F32)


def bytes_wait(ref, sem):
    pltpu.make_async_copy(ref, ref, sem).wait()


def row_iota(shape):
    return lax.broadcasted_iota(jnp.int32, shape, 0)


def pack(a):
    row = row_iota((8, 128))
    halves = []
    for h in range(2):
        t = a[:, 512 * h : 512 * h + 128]
        for q in range(1, 4):
            piece = a[:, 512 * h + 128 * q : 512 * h + 128 * (q + 1)]
            t = jnp.where(row // 2 == q, pltpu.roll(piece, 2 * q, 0), t)
        halves.append(t)
    return halves


def unpack(lo, hi):
    out = []
    for h in (lo, hi):
        for q in range(4):
            out.append(h if q == 0 else pltpu.roll(h, 8 - 2 * q, 0))
    return out


def times_minus_i(t, f):
    even = row_iota((8, 128)) % 2 == 0
    return jnp.where(even, f * pltpu.roll(t, 7, 0), -f * pltpu.roll(t, 1, 0))


def kernel(
    ham_hbm, surf, cloc, outer, v0, lmom,
    out_ref, inner_ref,
    hamv, opad, ut, u, uh, call, total, fin,
    vsend, vrec, ysend, yrec, itot, gsend, grec, esend, erec, strip, stot, strec,
    ham_sem, vs_sem, vr_sem, ys_sem, yr_sem, gs_sem, gr_sem, es_sem, er_sem, ss_sem, sr_sem,
    hs_sem, hr_sem, us_sem, ur_sem, cs_sem, cr_sem, fs_sem, fr_sem, loc_sem,
):
    r, c = lax.axis_index("radial"), lax.axis_index("chan")
    z, x, core = r // 8, lax.rem(r, 8) // 2, lax.rem(r, 2)
    is_root = r == 0
    self_plane = c == z
    up, down = lax.rem(r + 1, NRAD), lax.rem(r + NRAD - 1, NRAD)

    zero_rows = jnp.zeros((4, 64, 1920), BF16)
    hamv[:, 0:64, :] = zero_rows
    hamv[:, ROWS:RP, :] = zero_rows

    def ham_copy(i):
        return pltpu.make_async_copy(
            ham_hbm.at[:, pl.ds(1920 * i, 1920)],
            hamv.at[i, pl.ds(pl.multiple_of(64 * core, 64), ROWS)],
            ham_sem.at[i],
        )

    for i in range(4):
        ham_copy(i).start()

    barrier = pltpu.get_barrier_semaphore()

    def greet(device):
        pl.semaphore_signal(barrier, inc=1, device_id=device, device_id_type=MESH)

    for i in range(8):
        for y in range(NCH):
            producer = 8 * c + i

            @pl.when(jnp.logical_or(producer != r, c != y))
            def _():
                greet((producer, y))

    for d in range(1, NCH):
        greet((r, lax.rem(c + d, NCH)))
    greet((up, c))
    greet((down, c))

    @pl.when(is_root)
    def _():
        for d in range(1, NRAD):
            greet((d, c))

    @pl.when(jnp.logical_not(is_root))
    def _():
        greet((0, c))

    opad[:, 256:CP, :] = jnp.zeros((2, CP - 256, PTS), F32)
    opad[:, 0:LC, :] = outer[...]
    for s in range(2):
        for cb in range(3):
            for pb in range(2):
                ut[s, HALO + 128 * pb : HALO + 128 * (pb + 1), 128 * cb : 128 * (cb + 1)] = opad[
                    s, 128 * cb : 128 * (cb + 1), 128 * pb : 128 * (pb + 1)
                ].T
    u[:, :, 0:8, :] = jnp.zeros((NCH, 2, 8, CP), F32)
    u[:, :, 104:112, :] = jnp.zeros((NCH, 2, 8, CP), F32)
    for i in range(NCH):
        call[i, CR:CP, :] = jnp.zeros((CP - CR, NCH * CP), BF16)
    total[...] = jnp.zeros_like(total)
    itot[...] = jnp.zeros_like(itot)

    greeted = 37 - self_plane.astype(jnp.int32) + jnp.where(is_root, NRAD - 1, 1)
    pl.semaphore_wait(barrier, greeted)

    def send_term(k, lo, hi, inner):
        ps, slot = lax.rem(k, 2), lax.rem(k, SLOTS)

        @pl.when(k >= 2)
        def _():
            bytes_wait(yrec.at[0, pl.ds(0, 3)], ys_sem.at[ps])

            @pl.when(self_plane)
            def _():
                bytes_wait(vrec.at[0, pl.ds(0, 31)], vs_sem.at[ps])

            @pl.when(jnp.logical_not(self_plane))
            def _():
                bytes_wait(vrec.at[0], vs_sem.at[ps])

        both = jnp.concatenate([lo, hi], axis=0)
        ysend[ps] = both
        yrec[slot, c] = both

        def send_rows():
            vsend[ps] = both.astype(BF16)
            place = vrec.at[slot, 8 * x + 4 * core + c]

            def remote(rr):
                pltpu.make_async_remote_copy(
                    src_ref=vsend.at[ps],
                    dst_ref=place,
                    send_sem=vs_sem.at[ps],
                    recv_sem=vr_sem.at[slot, x],
                    device_id=(rr, z),
                    device_id_type=MESH,
                ).start()

            for dz in (2, 1, 3, 0):
                for dx in (2, 1, 3, 0):
                    for dc in (1, 0):
                        rr = 8 * lax.rem(z + dz, 4) + 2 * lax.rem(x + dx, 4) + lax.rem(core + dc, 2)
                        if dz or dx or dc:
                            remote(rr)
                        else:

                            @pl.when(self_plane)
                            def _():
                                pltpu.make_async_copy(vsend.at[ps], place, vr_sem.at[slot, x]).start()

                            @pl.when(jnp.logical_not(self_plane))
                            def _():
                                remote(rr)

        def send_peers():
            for d in (2, 1, 3):
                pltpu.make_async_remote_copy(
                    src_ref=ysend.at[ps],
                    dst_ref=yrec.at[slot, c],
                    send_sem=ys_sem.at[ps],
                    recv_sem=yr_sem.at[slot],
                    device_id=(r, lax.rem(c + d, NCH)),
                    device_id_type=MESH,
                ).start()

        send_peers()
        if inner is True:
            send_rows()
        else:
            pl.when(inner)(send_rows)

    def send_edge(k, rows):
        slot = lax.rem(k, SLOTS)
        for i in range(4):
            erec[slot, i : i + 1, :] = rows[i]
        for d in range(1, NRAD):
            pltpu.make_async_remote_copy(
                src_ref=erec.at[slot],
                dst_ref=erec.at[slot],
                send_sem=es_sem.at[slot],
                recv_sem=er_sem.at[slot],
                device_id=((d * 11) % NRAD, c),
                device_id_type=MESH,
            ).start()

    def send_strip(k):
        slot = lax.rem(k, SLOTS)
        for s in range(2):
            strec[slot, c, STRIP * s : STRIP * (s + 1), :] = strip[s, 8 : 8 + STRIP, :].astype(BF16)
        for d in (2, 1, 3):
            pltpu.make_async_remote_copy(
                src_ref=strec.at[slot, c],
                dst_ref=strec.at[slot, c],
                send_sem=ss_sem.at[slot],
                recv_sem=sr_sem.at[slot],
                device_id=(0, lax.rem(c + d, NCH)),
                device_id_type=MESH,
            ).start()

    lo, hi = pack(v0[...] * 0.25)
    send_term(0, lo, hi, True)

    @pl.when(is_root)
    def _():
        strip[...] = jnp.zeros_like(strip)
        for s in range(2):
            strip[s, 8 : 8 + STRIP, :] = ut[s, HALO : HALO + STRIP, :]
        stot[...] = jnp.zeros_like(stot)
        send_edge(0, [strip[s, 8 + m : 9 + m, :] for m in range(2) for s in range(2)])
        send_strip(0)

    def halo_copies():
        low = pltpu.make_async_remote_copy(
            src_ref=ut.at[:, pl.ds(HALO, HALO)], dst_ref=ut.at[:, pl.ds(HALO + PTS, HALO)],
            send_sem=hs_sem.at[0], recv_sem=hr_sem.at[0], device_id=(down, c), device_id_type=MESH,
        )
        high = pltpu.make_async_remote_copy(
            src_ref=ut.at[:, pl.ds(PTS, HALO)], dst_ref=ut.at[:, pl.ds(0, HALO)],
            send_sem=hs_sem.at[1], recv_sem=hr_sem.at[1], device_id=(up, c), device_id_type=MESH,
        )
        return low, high

    for cp in halo_copies():
        cp.start()

    def block_copy(d):
        cc = lax.rem(c + d, NCH)
        return pltpu.make_async_remote_copy(
            src_ref=ut.at[:, pl.ds(pl.multiple_of(BLK * cc, BLK), BLK + 2 * HALO)],
            dst_ref=u.at[c, :, pl.ds(8, BLK + 2 * HALO)],
            send_sem=us_sem.at[d - 1], recv_sem=ur_sem.at[d - 1],
            device_id=(r, cc), device_id_type=MESH,
        )

    def coupling_copy(d):
        return pltpu.make_async_remote_copy(
            src_ref=cloc.at[pl.ds(0, CR)],
            dst_ref=call.at[c, pl.ds(0, CR)],
            send_sem=cs_sem.at[d - 1], recv_sem=cr_sem.at[d - 1],
            device_id=(r, lax.rem(c + d, NCH)), device_id_type=MESH,
        )

    def final_copy(d):
        cc = lax.rem(c + d, NCH)
        return pltpu.make_async_remote_copy(
            src_ref=total.at[cc], dst_ref=fin.at[c],
            send_sem=fs_sem.at[d - 1], recv_sem=fr_sem.at[d - 1],
            device_id=(r, cc), device_id_type=MESH,
        )

    def own_block():
        return ut[:, pl.ds(pl.multiple_of(BLK * c, BLK), BLK + 2 * HALO), :]

    def outer_step(k):
        f = time_step / lax.convert_element_type(k, F32)
        for cp in range(NCH):
            for s in range(2):
                uh[cp, 96 * s : 96 * (s + 1), :] = u[cp, s, 8:104, :].astype(BF16)
        point = PTS * r + BLK * c - HALO + row_iota((96, 1))
        valid = jnp.logical_and(point >= 0, point < NRAD * PTS)
        radius = inner_radius + grid_step * (point.astype(F32) + 1.0)
        inv = 1.0 / (radius * radius)

        def chunk(cc, _):
            mixed = jnp.zeros((192, CP), F32)
            for cp in range(NCH):
                mixed += nn_dot(uh[cp], call[cp, :, pl.ds(pl.multiple_of(CP * cc, CP), CP)])
            applied = []
            for s in range(2):
                w = u[cc, s, 8:104, :]
                lap = (
                    (u[cc, s, 6:102, :] + u[cc, s, 10:106, :])
                    - 16.0 * (u[cc, s, 7:103, :] + u[cc, s, 9:105, :])
                    + 30.0 * w
                )
                applied.append(
                    lap_gain * lap + (lmom[pl.ds(cc, 1), :] * inv) * w + radius * mixed[96 * s : 96 * (s + 1)]
                )
            new = (jnp.where(valid, f * applied[1], 0.0), jnp.where(valid, -f * applied[0], 0.0))
            for s in range(2):
                u[cc, s, 8:104, :] = new[s]
                total[cc, s] += new[s][HALO : HALO + BLK]
            return 0

        lax.fori_loop(0, NCH, chunk, 0)

    def take_peers(k):
        slot = lax.rem(k, SLOTS)
        bytes_wait(yrec.at[slot, pl.ds(0, 3)], yr_sem.at[slot])
        own = (yrec[slot, 0] + yrec[slot, 1]) + (yrec[slot, 2] + yrec[slot, 3])
        itot[...] += own
        return own

    def step(k, _):
        ps, slot, before = lax.rem(k, 2), lax.rem(k, SLOTS), lax.rem(k + SLOTS - 1, SLOTS)
        f = time_step / lax.convert_element_type(k, F32)

        own = take_peers(k - 1)
        rows = jnp.concatenate(unpack(own[0:8], own[8:16]), axis=1).astype(BF16)
        g0, g1 = nt_dot(rows, surf[0]), nt_dot(rows, surf[1])
        ghost = jnp.where(row_iota((8, CP)) < 2, g0, pltpu.roll(g1, 2, 0))[0:4]

        @pl.when(is_root)
        def _():
            grec[slot, 0] = ghost

        @pl.when(jnp.logical_not(is_root))
        def _():
            @pl.when(k >= 3)
            def _():
                bytes_wait(grec.at[0, 0], gs_sem.at[ps])

            gsend[ps] = ghost
            pltpu.make_async_remote_copy(
                src_ref=gsend.at[ps], dst_ref=grec.at[slot, r],
                send_sem=gs_sem.at[ps], recv_sem=gr_sem.at[slot],
                device_id=(0, c), device_id_type=MESH,
            ).start()

        acc = jnp.zeros((8, RP), F32)
        for off in (0, 1, 3, 2):
            xi = lax.rem(x + off, 4)
            bytes_wait(vrec.at[before, pl.ds(8 * xi, 8)], vr_sem.at[before, xi])

            @pl.when(k == 1)
            def _():
                pltpu.make_async_copy(ham_hbm.at[:, pl.ds(0, 1920)], hamv.at[0, pl.ds(0, ROWS)], ham_sem.at[xi]).wait()

            tiles = []
            for co in range(2):
                parts = [vrec[before, 8 * xi + 4 * co + y].astype(F32) for y in range(NCH)]
                both = (parts[0] + parts[1]) + (parts[2] + parts[3])
                tiles.append(unpack(both[0:8], both[8:16]))
            lanes = tiles[0][:7] + [tiles[0][7] + tiles[1][0]] + tiles[1][1:]
            lhs = jnp.concatenate(lanes, axis=1).astype(BF16)
            acc += nt_dot(lhs, hamv[xi])

        @pl.when(jnp.logical_not(is_root))
        def _():
            bytes_wait(erec.at[before], er_sem.at[before])

        edge = jnp.concatenate([erec[before], jnp.zeros((4, CP), F32)], axis=0).astype(BF16)
        acc += surface_gain * (nn_dot(edge, surf[0]) + pltpu.roll(nn_dot(edge, surf[1]), 6, 0))
        lo, hi = pack(acc)
        send_term(k, times_minus_i(lo, f), times_minus_i(hi, f), k < ORDER)

        @pl.when(is_root)
        def _():
            bytes_wait(strec.at[before, pl.ds(0, 3)], sr_sem.at[before])
            mixed = jnp.zeros((2 * STRIP, CP), F32)
            for cp in range(NCH):
                mixed += nt_dot(strec[before, cp], cloc[:, CP * cp : CP * (cp + 1)])
            bytes_wait(grec.at[slot, pl.ds(0, NRAD - 1)], gr_sem.at[slot])
            seen = jnp.zeros((4, CP), F32)
            for i in range(NRAD):
                seen += grec[slot, i]
            for s in range(2):
                strip[s, 7:8, :] = seen[s : s + 1]
                strip[s, 6:7, :] = seen[2 + s : 3 + s]
            radius = inner_radius + grid_step * (row_iota((STRIP, 1)).astype(F32) + 1.0)
            inv = 1.0 / (radius * radius)
            applied = []
            for s in range(2):
                w = strip[s, 8 : 8 + STRIP, :]
                lap = (
                    (strip[s, 6 : 6 + STRIP, :] + strip[s, 10 : 10 + STRIP, :])
                    - 16.0 * (strip[s, 7 : 7 + STRIP, :] + strip[s, 9 : 9 + STRIP, :])
                    + 30.0 * w
                )
                applied.append(
                    lap_gain * lap + (lmom[pl.ds(c, 1), :] * inv) * w + radius * mixed[STRIP * s : STRIP * (s + 1)]
                )
            new = (f * applied[1], -f * applied[0])
            for s in range(2):
                strip[s, 8 : 8 + STRIP, :] = new[s]
                stot[s] += new[s]
            bytes_wait(strec.at[0, pl.ds(0, 3)], ss_sem.at[before])
            bytes_wait(grec.at[0, pl.ds(0, NRAD - 1)], es_sem.at[before])

            @pl.when(k < ORDER)
            def _():
                send_edge(k, [new[s][m : m + 1] for m in range(2) for s in range(2)])
                send_strip(k)

        @pl.when(k == 1)
        def _():
            for cp in halo_copies():
                cp.wait()

            @pl.when(r == NRAD - 1)
            def _():
                ut[:, HALO + PTS :, :] = jnp.zeros((2, HALO, CP), F32)

            for d in (2, 1, 3):
                block_copy(d).start()
            for d in (2, 1, 3):
                coupling_copy(d).start()
            u[c, :, 8:104, :] = own_block()
            call[c, 0:CR, :] = cloc[0:CR, :]

        return 0

    lax.fori_loop(1, ORDER + 1, step, 0)

    for d in (1, 2, 3):
        block_copy(d).wait()
    for d in (1, 2, 3):
        coupling_copy(d).wait()

    def outer_loop(k, _):
        outer_step(k)
        return 0

    lax.fori_loop(1, ORDER + 1, outer_loop, 0)
    for d in (2, 1, 3):
        final_copy(d).start()
    fin[c] = total[c]
    take_peers(ORDER)
    inner_ref[...] = jnp.concatenate(unpack(itot[0:8], itot[8:16]), axis=1)
    for d in (1, 2, 3):
        final_copy(d).wait()

    @pl.when(is_root)
    def _():
        for s in range(2):
            fin[0, s, 0:HALO, :] = stot[s, 0:HALO, :]

    for s in range(2):
        for pb in range(2):
            rows = jnp.concatenate([fin[2 * pb, s], fin[2 * pb + 1, s]], axis=0)
            for cb in range(3):
                n = min(128, LC - 128 * cb)
                out_ref[s, 128 * cb : 128 * cb + n, 128 * pb : 128 * (pb + 1)] = (
                    outer[s, 128 * cb : 128 * cb + n, 128 * pb : 128 * (pb + 1)]
                    + rows[:, 128 * cb : 128 * (cb + 1)].T[0:n]
                )

    @pl.when(self_plane)
    def _():
        bytes_wait(vrec.at[0, pl.ds(0, 31)], vs_sem.at[(ORDER - 1) % 2])

    @pl.when(jnp.logical_not(self_plane))
    def _():
        bytes_wait(vrec.at[0], vs_sem.at[(ORDER - 1) % 2])

    for k in (ORDER - 1, ORDER):
        bytes_wait(yrec.at[0, pl.ds(0, 3)], ys_sem.at[k % 2])

        @pl.when(jnp.logical_not(is_root))
        def _():
            bytes_wait(grec.at[0, 0], gs_sem.at[k % 2])


def local(outer_wave, inner_wave, inner_ham, surface, dipole, ang_mom, target, couple_mask):
    chan = lax.axis_index("chan")
    core = lax.rem(lax.axis_index("radial"), 2)
    pad_c = ((0, 0), (0, CP - LC))
    mom = jnp.pad(ang_mom.reshape(NCH, LC), pad_c, constant_values=-9)
    tgt = jnp.pad(target.reshape(NCH, LC), pad_c, constant_values=-1)
    levels = jnp.arange(couple_mask.shape[0])
    hot = (tgt.reshape(-1)[:, None] == levels[None, :]).astype(BF16)
    hot_mine = lax.dynamic_slice_in_dim(hot, chan * CP, CP, 0)
    allowed = nn_dot(nn_dot(hot_mine, couple_mask.astype(BF16)).astype(BF16), hot.T)
    mom_mine = lax.dynamic_slice_in_dim(mom.reshape(-1), chan * CP, CP, 0)
    step_l = jnp.abs(mom_mine[:, None] - mom.reshape(-1)[None, :]) == 1
    dip = jnp.pad(dipole.reshape(LC, NCH, LC), ((0, CP - LC), (0, 0), (0, CP - LC))).reshape(CP, NCH * CP)
    cloc = jnp.where(step_l & (allowed > 0.5), dip, jnp.zeros_like(dip))
    lvals = mom.astype(F32)
    lmom = jnp.where(mom >= 0, lvals * (lvals + 1.0) / 2.0, 0.0)
    shift = RP - ROWS

    def shifted(a, *front):
        return jnp.where(
            core == 1, jnp.pad(a, front + ((shift, 0),)), jnp.pad(a, front + ((0, shift),))
        )

    surf = shifted(surface, (0, 0), (0, CP - LC))
    v0 = shifted(inner_wave, (0, 6))

    vm = pl.BlockSpec(memory_space=pltpu.VMEM)
    dma = pltpu.SemaphoreType.DMA
    out, inner = pl.pallas_call(
        kernel,
        out_shape=(
            jax.ShapeDtypeStruct((2, LC, PTS), F32),
            jax.ShapeDtypeStruct((8, RP), F32),
        ),
        in_specs=[pl.BlockSpec(memory_space=pl.ANY)] + [vm] * 5,
        out_specs=(vm, vm),
        scratch_shapes=[
            pltpu.VMEM((4, RP, 1920), BF16),
            pltpu.VMEM((2, CP, PTS), F32),
            pltpu.VMEM((2, PTS + 2 * HALO, CP), F32),
            pltpu.VMEM((NCH, 2, 112, CP), F32),
            pltpu.VMEM((NCH, 192, CP), BF16),
            pltpu.VMEM((NCH, CP, NCH * CP), BF16),
            pltpu.VMEM((NCH, 2, BLK, CP), F32),
            pltpu.VMEM((NCH, 2, BLK, CP), F32),
            pltpu.VMEM((2, 16, 128), BF16),
            pltpu.VMEM((SLOTS, 32, 16, 128), BF16),
            pltpu.VMEM((2, 16, 128), F32),
            pltpu.VMEM((SLOTS, NCH, 16, 128), F32),
            pltpu.VMEM((16, 128), F32),
            pltpu.VMEM((2, 4, CP), F32),
            pltpu.VMEM((SLOTS, NRAD, 4, CP), F32),
            pltpu.VMEM((2, 4, CP), F32),
            pltpu.VMEM((SLOTS, 4, CP), F32),
            pltpu.VMEM((2, 48, CP), F32),
            pltpu.VMEM((2, STRIP, CP), F32),
            pltpu.VMEM((SLOTS, NCH, 2 * STRIP, CP), BF16),
            dma((4,)),
            dma((2,)), dma((SLOTS, 4)),
            dma((2,)), dma((SLOTS,)),
            dma((2,)), dma((SLOTS,)),
            dma((SLOTS,)), dma((SLOTS,)),
            dma((SLOTS,)), dma((SLOTS,)),
            dma((2,)), dma((2,)),
            dma((3,)), dma((3,)),
            dma((3,)), dma((3,)),
            dma((3,)), dma((3,)),
            dma((1,)),
        ],
        compiler_params=pltpu.CompilerParams(
            collective_id=0, has_side_effects=True, vmem_limit_bytes=58 * 2**20
        ),
    )(inner_ham, surf, cloc, outer_wave, v0, lmom)
    inner_next = lax.dynamic_slice(inner, (0, shift * core), (2, ROWS))
    return out, inner_next


def solution(mesh):
    placed = (
        P(None, "chan", "radial"),
        P(None, "radial"),
        P("radial", "chan"),
        P(None, "chan", "radial"),
        P("chan", None),
        P(),
        P(),
        P(),
    )
    return jax.shard_map(
        local,
        mesh=mesh,
        in_specs=placed,
        out_specs=(P(None, "chan", "radial"), P(None, "radial")),
        check_vma=False,
    )
```

```python
import jax
import jax.numpy as jnp
from jax import lax
from jax.experimental import pallas as pl
from jax.experimental.pallas import tpu as pltpu
from jax.sharding import PartitionSpec as P

ORDER = 8
time_step = 0.008
grid_step = 0.08
inner_radius = 20.0
surface_gain = 16.0 / (24.0 * grid_step * grid_step)
lap_gain = 1.0 / (24.0 * grid_step * grid_step)

MESH = pl.DeviceIdType.MESH
F32, BF16 = jnp.float32, jnp.bfloat16
NRAD, NCH = 32, 4
ROWS, LC, PTS = 960, 300, 256
RP, CP = 1024, 384
SLOTS = 4
HALO, BLK = 16, 64
CR = 320
STRIP = 32
NT = (((1,), (1,)), ((), ()))


def nt_dot(a, b):
    return lax.dot_general(a, b, NT, preferred_element_type=F32)


def nn_dot(a, b):
    return jnp.dot(a, b, preferred_element_type=F32)


def bytes_wait(ref, sem):
    pltpu.make_async_copy(ref, ref, sem).wait()


def row_iota(shape):
    return lax.broadcasted_iota(jnp.int32, shape, 0)


def pack(a):
    row = row_iota((8, 128))
    halves = []
    for h in range(2):
        t = a[:, 512 * h : 512 * h + 128]
        for q in range(1, 4):
            piece = a[:, 512 * h + 128 * q : 512 * h + 128 * (q + 1)]
            t = jnp.where(row // 2 == q, pltpu.roll(piece, 2 * q, 0), t)
        halves.append(t)
    return halves


def unpack(lo, hi):
    out = []
    for h in (lo, hi):
        for q in range(4):
            out.append(h if q == 0 else pltpu.roll(h, 8 - 2 * q, 0))
    return out


def times_minus_i(t, f):
    even = row_iota((8, 128)) % 2 == 0
    return jnp.where(even, f * pltpu.roll(t, 7, 0), -f * pltpu.roll(t, 1, 0))


def kernel(
    ham_hbm, surf, cloc, outer, v0, lmom,
    out_ref, inner_ref,
    stage, hamt, opad, ut, u, uh, call, total, fin,
    vsend, vrec, ysend, yrec, itot, term, gsend, grec, erec, strip, stot, strec,
    ham_sem, vs_sem, vr_sem, ys_sem, yr_sem, gs_sem, gr_sem, es_sem, er_sem, ss_sem, sr_sem,
    hs_sem, hr_sem, us_sem, ur_sem, cs_sem, cr_sem, ds_sem, dr_sem, fs_sem, fr_sem,
):
    r, c = lax.axis_index("radial"), lax.axis_index("chan")
    z, x, core = r // 8, lax.rem(r, 8) // 2, lax.rem(r, 2)
    is_root = r == 0
    self_plane = c == z
    up, down = lax.rem(r + 1, NRAD), lax.rem(r + NRAD - 1, NRAD)

    zero_rows = jnp.zeros((4, 64, 1920), BF16)
    stage[:, 0:64, :] = zero_rows
    stage[:, ROWS:RP, :] = zero_rows

    def ham_copy(i):
        return pltpu.make_async_copy(
            ham_hbm.at[:, pl.ds(1920 * i, 1920)],
            stage.at[i, pl.ds(pl.multiple_of(64 * core, 64), ROWS)],
            ham_sem.at[i],
        )

    for i in range(4):
        ham_copy(i).start()

    barrier = pltpu.get_barrier_semaphore()

    def greet(device):
        pl.semaphore_signal(barrier, inc=1, device_id=device, device_id_type=MESH)

    for i in range(8):
        producer = 8 * c + i

        @pl.when(producer != r)
        def _():
            greet((producer, c))

    for d in range(1, NCH):
        greet((r, lax.rem(c + d, NCH)))
    greet((up, c))
    greet((down, c))

    @pl.when(is_root)
    def _():
        for d in range(1, NRAD):
            greet((d, c))

    @pl.when(jnp.logical_not(is_root))
    def _():
        greet((0, c))

    opad[:, 256:CP, :] = jnp.zeros((2, CP - 256, PTS), F32)
    opad[:, 0:LC, :] = outer[...]
    for s in range(2):
        for cb in range(3):
            for pb in range(2):
                ut[s, HALO + 128 * pb : HALO + 128 * (pb + 1), 128 * cb : 128 * (cb + 1)] = opad[
                    s, 128 * cb : 128 * (cb + 1), 128 * pb : 128 * (pb + 1)
                ].T
    u[:, :, 0:8, :] = jnp.zeros((NCH, 2, 8, CP), F32)
    u[:, :, 104:112, :] = jnp.zeros((NCH, 2, 8, CP), F32)
    for i in range(NCH):
        call[i, CR:CP, :] = jnp.zeros((CP - CR, NCH * CP), BF16)
    call[c, 0:CR, :] = cloc[0:CR, :]
    total[...] = jnp.zeros_like(total)

    greeted = 5 + jnp.where(self_plane, NRAD - 1, 0) + jnp.where(is_root, NRAD - 1, 1)
    pl.semaphore_wait(barrier, greeted)

    def send_term(k, lo, hi):
        ps, slot = lax.rem(k, 2), lax.rem(k, SLOTS)

        @pl.when(k >= 3)
        def _():
            bytes_wait(yrec.at[0, pl.ds(0, 3)], ys_sem.at[ps])

        both = jnp.concatenate([lo, hi], axis=0)
        ysend[ps] = both
        yrec[slot, c] = both
        for d in (2, 1, 3):
            pltpu.make_async_remote_copy(
                src_ref=ysend.at[ps],
                dst_ref=yrec.at[slot, c],
                send_sem=ys_sem.at[ps],
                recv_sem=yr_sem.at[slot],
                device_id=(r, lax.rem(c + d, NCH)),
                device_id_type=MESH,
            ).start()

    def spread(k):
        ps, slot = lax.rem(k, 2), lax.rem(k + SLOTS - 1, SLOTS)

        @pl.when(k >= 3)
        def _():
            bytes_wait(vrec.at[0, pl.ds(0, 31)], vs_sem.at[ps])

        vsend[ps] = term[...].astype(BF16)
        place = vrec.at[slot, 2 * x + core]
        for dz in (2, 1, 3, 0):
            for dx in (2, 1, 3, 0):
                for dc in (1, 0):
                    if dz or dx or dc:
                        rr = 8 * lax.rem(z + dz, 4) + 2 * lax.rem(x + dx, 4) + lax.rem(core + dc, 2)
                        pltpu.make_async_remote_copy(
                            src_ref=vsend.at[ps],
                            dst_ref=place,
                            send_sem=vs_sem.at[ps],
                            recv_sem=vr_sem.at[slot, x],
                            device_id=(rr, c),
                            device_id_type=MESH,
                        ).start()
        pltpu.make_async_copy(vsend.at[ps], place, vr_sem.at[slot, x]).start()

    def send_edge(k, rows):
        slot = lax.rem(k, SLOTS)
        for i in range(4):
            erec[slot, i : i + 1, :] = rows[i]
        for d in range(1, NRAD):
            pltpu.make_async_remote_copy(
                src_ref=erec.at[slot],
                dst_ref=erec.at[slot],
                send_sem=es_sem.at[slot],
                recv_sem=er_sem.at[slot],
                device_id=((d * 11) % NRAD, c),
                device_id_type=MESH,
            ).start()

    def send_strip(k):
        slot = lax.rem(k, SLOTS)
        for s in range(2):
            strec[slot, c, STRIP * s : STRIP * (s + 1), :] = strip[s, 8 : 8 + STRIP, :].astype(BF16)
        for d in (2, 1, 3):
            pltpu.make_async_remote_copy(
                src_ref=strec.at[slot, c],
                dst_ref=strec.at[slot, c],
                send_sem=ss_sem.at[slot],
                recv_sem=sr_sem.at[slot],
                device_id=(0, lax.rem(c + d, NCH)),
                device_id_type=MESH,
            ).start()

    lo, hi = pack(v0[...])
    term[...] = jnp.concatenate([lo, hi], axis=0)
    itot[...] = term[...]

    @pl.when(is_root)
    def _():
        strip[...] = jnp.zeros_like(strip)
        for s in range(2):
            strip[s, 8 : 8 + STRIP, :] = ut[s, HALO : HALO + STRIP, :]
        stot[...] = jnp.zeros_like(stot)
        send_edge(0, [strip[s, 8 + m : 9 + m, :] for m in range(2) for s in range(2)])
        send_strip(0)

    def halo_copies():
        low = pltpu.make_async_remote_copy(
            src_ref=ut.at[:, pl.ds(HALO, HALO)], dst_ref=ut.at[:, pl.ds(HALO + PTS, HALO)],
            send_sem=hs_sem.at[0], recv_sem=hr_sem.at[0], device_id=(down, c), device_id_type=MESH,
        )
        high = pltpu.make_async_remote_copy(
            src_ref=ut.at[:, pl.ds(PTS, HALO)], dst_ref=ut.at[:, pl.ds(0, HALO)],
            send_sem=hs_sem.at[1], recv_sem=hr_sem.at[1], device_id=(up, c), device_id_type=MESH,
        )
        return low, high

    for cp in halo_copies():
        cp.start()

    def block_copy(d):
        cc = lax.rem(c + d, NCH)
        return pltpu.make_async_remote_copy(
            src_ref=ut.at[:, pl.ds(pl.multiple_of(BLK * cc, BLK), BLK + 2 * HALO)],
            dst_ref=u.at[c, :, pl.ds(8, BLK + 2 * HALO)],
            send_sem=us_sem.at[d - 1], recv_sem=ur_sem.at[d - 1],
            device_id=(r, cc), device_id_type=MESH,
        )

    half = pl.ds(pl.multiple_of(CR // 2 * core, CR // 2), CR // 2)

    def next_block(p, d):
        return lax.rem(p + (2 if d == 1 else 1), NCH)

    def columns(i):
        return pl.ds(pl.multiple_of(CP * i, CP), CP)

    def coupling_copies(d):
        out = []
        for j in range(2):
            cols = columns(c if j == 0 else next_block(c, d))
            out.append(
                pltpu.make_async_remote_copy(
                    src_ref=cloc.at[half, cols],
                    dst_ref=call.at[c, half, cols],
                    send_sem=cs_sem.at[2 * d - 2 + j], recv_sem=cr_sem.at[2 * d - 2 + j],
                    device_id=(r, lax.rem(c + d, NCH)), device_id_type=MESH,
                )
            )
        return out

    def share_copies(d):
        p = lax.rem(c + NCH - d, NCH)
        out = []
        for j in range(2):
            place = call.at[p, half, columns(p if j == 0 else next_block(p, d))]
            out.append(
                pltpu.make_async_remote_copy(
                    src_ref=place, dst_ref=place,
                    send_sem=ds_sem.at[2 * d - 2 + j], recv_sem=dr_sem.at[2 * d - 2 + j],
                    device_id=(r + 1 - 2 * core, c), device_id_type=MESH,
                )
            )
        return out

    def mirror(a, b):
        call[b, :, columns(a)] = call[a, :, columns(b)].T

    for d in (2, 1, 3):
        for cp in coupling_copies(d):
            cp.start()

    def final_copy(d):
        cc = lax.rem(c + d, NCH)
        return pltpu.make_async_remote_copy(
            src_ref=total.at[cc], dst_ref=fin.at[c],
            send_sem=fs_sem.at[d - 1], recv_sem=fr_sem.at[d - 1],
            device_id=(r, cc), device_id_type=MESH,
        )

    def own_block():
        return ut[:, pl.ds(pl.multiple_of(BLK * c, BLK), BLK + 2 * HALO), :]

    def outer_step(k):
        f = time_step / lax.convert_element_type(k, F32)
        for cp in range(NCH):
            for s in range(2):
                uh[cp, 96 * s : 96 * (s + 1), :] = u[cp, s, 8:104, :].astype(BF16)
        point = PTS * r + BLK * c - HALO + row_iota((96, 1))
        valid = jnp.logical_and(point >= 0, point < NRAD * PTS)
        radius = inner_radius + grid_step * (point.astype(F32) + 1.0)
        inv = 1.0 / (radius * radius)

        def chunk(cc, _):
            mixed = jnp.zeros((192, CP), F32)
            for cp in range(NCH):
                mixed += nn_dot(uh[cp], call[cp, :, pl.ds(pl.multiple_of(CP * cc, CP), CP)])
            applied = []
            for s in range(2):
                w = u[cc, s, 8:104, :]
                lap = (
                    (u[cc, s, 6:102, :] + u[cc, s, 10:106, :])
                    - 16.0 * (u[cc, s, 7:103, :] + u[cc, s, 9:105, :])
                    + 30.0 * w
                )
                applied.append(
                    lap_gain * lap + (lmom[pl.ds(cc, 1), :] * inv) * w + radius * mixed[96 * s : 96 * (s + 1)]
                )
            new = (jnp.where(valid, f * applied[1], 0.0), jnp.where(valid, -f * applied[0], 0.0))
            for s in range(2):
                u[cc, s, 8:104, :] = new[s]
                total[cc, s] += new[s][HALO : HALO + BLK]
            return 0

        lax.fori_loop(0, NCH, chunk, 0)

    first = 4

    def outer_when(k, start, index):
        @pl.when(jnp.logical_and(k >= start, k < start + 4))
        def _():
            outer_step(index)

    def step(k, _):
        ps, slot, before = lax.rem(k, 2), lax.rem(k, SLOTS), lax.rem(k + SLOTS - 1, SLOTS)
        f = time_step / lax.convert_element_type(k, F32)

        @pl.when(self_plane)
        def _():
            spread(k)

        rows = jnp.concatenate(unpack(term[0:8], term[8:16]), axis=1).astype(BF16)
        g0, g1 = nt_dot(rows, surf[0]), nt_dot(rows, surf[1])
        ghost = jnp.where(row_iota((8, CP)) < 2, g0, pltpu.roll(g1, 2, 0))[0:4]

        @pl.when(is_root)
        def _():
            grec[slot, 0] = ghost

        @pl.when(jnp.logical_not(is_root))
        def _():
            @pl.when(k >= 3)
            def _():
                bytes_wait(grec.at[0, 0], gs_sem.at[ps])

            gsend[ps] = ghost
            pltpu.make_async_remote_copy(
                src_ref=gsend.at[ps], dst_ref=grec.at[slot, r],
                send_sem=gs_sem.at[ps], recv_sem=gr_sem.at[slot],
                device_id=(0, c), device_id_type=MESH,
            ).start()

        @pl.when(k == 1)
        def _():
            for i in range(4):
                ham_copy(i).wait()

                def turn(j, _):
                    at = pl.ds(pl.multiple_of(128 * j, 128), 128)
                    hamt[i, at, :] = stage[i, :, at].T
                    return 0

                lax.fori_loop(0, 15, turn, 0)

        @pl.when(k == first - 1)
        def _():
            for d in (2, 1, 3):
                for cp in coupling_copies(d):
                    cp.wait()
                for cp in share_copies(d):
                    cp.start()

        @pl.when(k == first)
        def _():
            for d in (2, 1, 3):
                for cp in share_copies(d):
                    cp.wait()
            for d in (1, 2, 3):
                mirror(c, lax.rem(c + d, NCH))
                p = lax.rem(c + NCH - d, NCH)
                mirror(p, next_block(p, d))
                block_copy(d).wait()

        outer_when(k, first + 1, 2 * (k - first))

        @pl.when(k == first + 4)
        def _():
            for d in (2, 1, 3):
                final_copy(d).start()
            fin[c] = total[c]

        acc = jnp.zeros((8, RP), F32)
        for off in (0, 1, 3, 2):
            xi = lax.rem(x + off, 4)
            bytes_wait(vrec.at[before, pl.ds(2 * xi, 2)], vr_sem.at[before, xi])
            tiles = []
            for co in range(2):
                both = vrec[before, 2 * xi + co].astype(F32)
                tiles.append(unpack(both[0:8], both[8:16]))
            lanes = tiles[0][:7] + [tiles[0][7] + tiles[1][0]] + tiles[1][1:]
            lhs = jnp.concatenate(lanes, axis=1).astype(BF16)
            acc += nn_dot(lhs, hamt[xi])

        @pl.when(jnp.logical_not(is_root))
        def _():
            bytes_wait(erec.at[before], er_sem.at[before])

        edge = jnp.concatenate([erec[before], jnp.zeros((4, CP), F32)], axis=0).astype(BF16)
        acc += surface_gain * (nn_dot(edge, surf[0]) + pltpu.roll(nn_dot(edge, surf[1]), 6, 0))
        lo, hi = pack(acc)
        send_term(k, times_minus_i(lo, f), times_minus_i(hi, f))

        @pl.when(is_root)
        def _():
            bytes_wait(strec.at[before, pl.ds(0, 3)], sr_sem.at[before])
            mixed = jnp.zeros((2 * STRIP, CP), F32)
            for cp in range(NCH):
                mixed += nt_dot(strec[before, cp], cloc[:, CP * cp : CP * (cp + 1)])
            bytes_wait(grec.at[slot, pl.ds(0, NRAD - 1)], gr_sem.at[slot])
            seen = jnp.zeros((4, CP), F32)
            for i in range(NRAD):
                seen += grec[slot, i]
            for s in range(2):
                strip[s, 7:8, :] = seen[s : s + 1]
                strip[s, 6:7, :] = seen[2 + s : 3 + s]
            radius = inner_radius + grid_step * (row_iota((STRIP, 1)).astype(F32) + 1.0)
            inv = 1.0 / (radius * radius)
            applied = []
            for s in range(2):
                w = strip[s, 8 : 8 + STRIP, :]
                lap = (
                    (strip[s, 6 : 6 + STRIP, :] + strip[s, 10 : 10 + STRIP, :])
                    - 16.0 * (strip[s, 7 : 7 + STRIP, :] + strip[s, 9 : 9 + STRIP, :])
                    + 30.0 * w
                )
                applied.append(
                    lap_gain * lap + (lmom[pl.ds(c, 1), :] * inv) * w + radius * mixed[STRIP * s : STRIP * (s + 1)]
                )
            new = (f * applied[1], -f * applied[0])
            for s in range(2):
                strip[s, 8 : 8 + STRIP, :] = new[s]
                stot[s] += new[s]
            bytes_wait(strec.at[0, pl.ds(0, 3)], ss_sem.at[before])
            bytes_wait(grec.at[0, pl.ds(0, NRAD - 1)], es_sem.at[before])

            @pl.when(k < ORDER)
            def _():
                send_edge(k, [new[s][m : m + 1] for m in range(2) for s in range(2)])
                send_strip(k)

        @pl.when(k == 1)
        def _():
            for cp in halo_copies():
                cp.wait()

            @pl.when(r == NRAD - 1)
            def _():
                ut[:, HALO + PTS :, :] = jnp.zeros((2, HALO, CP), F32)

            for d in (2, 1, 3):
                block_copy(d).start()
            u[c, :, 8:104, :] = own_block()

        outer_when(k, first, 2 * (k - first) + 1)

        bytes_wait(yrec.at[slot, pl.ds(0, 3)], yr_sem.at[slot])
        own = (yrec[slot, 0] + yrec[slot, 1]) + (yrec[slot, 2] + yrec[slot, 3])
        itot[...] += own
        term[...] = own
        return 0

    lax.fori_loop(1, ORDER + 1, step, 0)

    inner_ref[...] = jnp.concatenate(unpack(itot[0:8], itot[8:16]), axis=1)
    for d in (1, 2, 3):
        final_copy(d).wait()

    @pl.when(is_root)
    def _():
        for s in range(2):
            fin[0, s, 0:HALO, :] = stot[s, 0:HALO, :]

    for s in range(2):
        for pb in range(2):
            rows = jnp.concatenate([fin[2 * pb, s], fin[2 * pb + 1, s]], axis=0)
            for cb in range(3):
                n = min(128, LC - 128 * cb)
                out_ref[s, 128 * cb : 128 * cb + n, 128 * pb : 128 * (pb + 1)] = (
                    outer[s, 128 * cb : 128 * cb + n, 128 * pb : 128 * (pb + 1)]
                    + rows[:, 128 * cb : 128 * (cb + 1)].T[0:n]
                )

    for k in (ORDER - 1, ORDER):
        bytes_wait(yrec.at[0, pl.ds(0, 3)], ys_sem.at[k % 2])

        @pl.when(self_plane)
        def _():
            bytes_wait(vrec.at[0, pl.ds(0, 31)], vs_sem.at[k % 2])

        @pl.when(jnp.logical_not(is_root))
        def _():
            bytes_wait(grec.at[0, 0], gs_sem.at[k % 2])


def local(outer_wave, inner_wave, inner_ham, surface, dipole, ang_mom, target, couple_mask):
    chan = lax.axis_index("chan")
    core = lax.rem(lax.axis_index("radial"), 2)
    pad_c = ((0, 0), (0, CP - LC))
    mom = jnp.pad(ang_mom.reshape(NCH, LC), pad_c, constant_values=-9)
    tgt = jnp.pad(target.reshape(NCH, LC), pad_c, constant_values=-1)
    levels = jnp.arange(couple_mask.shape[0])
    hot = (tgt.reshape(-1)[:, None] == levels[None, :]).astype(BF16)
    hot_mine = lax.dynamic_slice_in_dim(hot, chan * CP, CP, 0)
    allowed = nn_dot(nn_dot(hot_mine, couple_mask.astype(BF16)).astype(BF16), hot.T)
    mom_mine = lax.dynamic_slice_in_dim(mom.reshape(-1), chan * CP, CP, 0)
    step_l = jnp.abs(mom_mine[:, None] - mom.reshape(-1)[None, :]) == 1
    dip = jnp.pad(dipole.reshape(LC, NCH, LC), ((0, CP - LC), (0, 0), (0, CP - LC))).reshape(CP, NCH * CP)
    cloc = jnp.where(step_l & (allowed > 0.5), dip, jnp.zeros_like(dip))
    lvals = mom.astype(F32)
    lmom = jnp.where(mom >= 0, lvals * (lvals + 1.0) / 2.0, 0.0)
    shift = RP - ROWS

    def shifted(a, *front):
        return jnp.where(
            core == 1, jnp.pad(a, front + ((shift, 0),)), jnp.pad(a, front + ((0, shift),))
        )

    surf = shifted(surface, (0, 0), (0, CP - LC))
    v0 = shifted(inner_wave, (0, 6))

    vm = pl.BlockSpec(memory_space=pltpu.VMEM)
    dma = pltpu.SemaphoreType.DMA
    out, inner = pl.pallas_call(
        kernel,
        out_shape=(
            jax.ShapeDtypeStruct((2, LC, PTS), F32),
            jax.ShapeDtypeStruct((8, RP), F32),
        ),
        in_specs=[pl.BlockSpec(memory_space=pl.ANY)] + [vm] * 5,
        out_specs=(vm, vm),
        scratch_shapes=[
            pltpu.VMEM((4, RP, 1920), BF16),
            pltpu.VMEM((4, 1920, RP), BF16),
            pltpu.VMEM((2, CP, PTS), F32),
            pltpu.VMEM((2, PTS + 2 * HALO, CP), F32),
            pltpu.VMEM((NCH, 2, 112, CP), F32),
            pltpu.VMEM((NCH, 192, CP), BF16),
            pltpu.VMEM((NCH, CP, NCH * CP), BF16),
            pltpu.VMEM((NCH, 2, BLK, CP), F32),
            pltpu.VMEM((NCH, 2, BLK, CP), F32),
            pltpu.VMEM((2, 16, 128), BF16),
            pltpu.VMEM((SLOTS, 32, 16, 128), BF16),
            pltpu.VMEM((2, 16, 128), F32),
            pltpu.VMEM((SLOTS, NCH, 16, 128), F32),
            pltpu.VMEM((16, 128), F32),
            pltpu.VMEM((16, 128), F32),
            pltpu.VMEM((2, 4, CP), F32),
            pltpu.VMEM((SLOTS, NRAD, 4, CP), F32),
            pltpu.VMEM((SLOTS, 4, CP), F32),
            pltpu.VMEM((2, 48, CP), F32),
            pltpu.VMEM((2, STRIP, CP), F32),
            pltpu.VMEM((SLOTS, NCH, 2 * STRIP, CP), BF16),
            dma((4,)),
            dma((2,)), dma((SLOTS, 4)),
            dma((2,)), dma((SLOTS,)),
            dma((2,)), dma((SLOTS,)),
            dma((SLOTS,)), dma((SLOTS,)),
            dma((SLOTS,)), dma((SLOTS,)),
            dma((2,)), dma((2,)),
            dma((3,)), dma((3,)),
            dma((6,)), dma((6,)),
            dma((6,)), dma((6,)),
            dma((3,)), dma((3,)),
        ],
        compiler_params=pltpu.CompilerParams(
            collective_id=0, has_side_effects=True, vmem_limit_bytes=58 * 2**20
        ),
    )(inner_ham, surf, cloc, outer_wave, v0, lmom)
    inner_next = lax.dynamic_slice(inner, (0, shift * core), (2, ROWS))
    return out, inner_next


def solution(mesh):
    placed = (
        P(None, "chan", "radial"),
        P(None, "radial"),
        P("radial", "chan"),
        P(None, "chan", "radial"),
        P("chan", None),
        P(),
        P(),
        P(),
    )
    return jax.shard_map(
        local,
        mesh=mesh,
        in_specs=placed,
        out_specs=(P(None, "chan", "radial"), P(None, "radial")),
        check_vma=False,
    )
```

```python
import jax
import jax.numpy as jnp
from jax import lax
from jax.experimental import pallas as pl
from jax.experimental.pallas import tpu as pltpu
from jax.sharding import PartitionSpec as P

ORDER = 8
time_step = 0.008
grid_step = 0.08
inner_radius = 20.0
surface_gain = 16.0 / (24.0 * grid_step * grid_step)
lap_gain = 1.0 / (24.0 * grid_step * grid_step)

MESH = pl.DeviceIdType.MESH
F32, BF16 = jnp.float32, jnp.bfloat16
NRAD, NCH = 32, 4
ROWS, LC, PTS = 960, 300, 256
RP, CP = 1024, 384
SLOTS = 4
HALO, BLK = 16, 64
CR = 320
STRIP = 32
NT = (((1,), (1,)), ((), ()))


def nt_dot(a, b):
    return lax.dot_general(a, b, NT, preferred_element_type=F32)


def nn_dot(a, b):
    return jnp.dot(a, b, preferred_element_type=F32)


def bytes_wait(ref, sem):
    pltpu.make_async_copy(ref, ref, sem).wait()


def row_iota(shape):
    return lax.broadcasted_iota(jnp.int32, shape, 0)


def pack(a):
    row = row_iota((8, 128))
    halves = []
    for h in range(2):
        t = a[:, 512 * h : 512 * h + 128]
        for q in range(1, 4):
            piece = a[:, 512 * h + 128 * q : 512 * h + 128 * (q + 1)]
            t = jnp.where(row // 2 == q, pltpu.roll(piece, 2 * q, 0), t)
        halves.append(t)
    return halves


def unpack(lo, hi):
    out = []
    for h in (lo, hi):
        for q in range(4):
            out.append(h if q == 0 else pltpu.roll(h, 8 - 2 * q, 0))
    return out


def times_minus_i(t, f):
    even = row_iota((8, 128)) % 2 == 0
    return jnp.where(even, f * pltpu.roll(t, 7, 0), -f * pltpu.roll(t, 1, 0))


def kernel(
    ham_hbm, surf_in, dipole, outer, v0, mom, target, couple_mask,
    out_ref, inner_ref,
    surf, cloc, dpad, pads, hot, lmom, m64, v0p, stage, hamt, opad, ut, u, uh, mix, call, total, fin,
    vsend, vrec, ysend, yrec, itot, term, gsend, grec, erec, strip, stot, strec,
    ham_sem, vs_sem, vr_sem, ys_sem, yr_sem, gs_sem, gr_sem, es_sem, er_sem, ss_sem, sr_sem,
    hs_sem, hr_sem, us_sem, ur_sem, cs_sem, cr_sem, ds_sem, dr_sem, fs_sem, fr_sem,
):
    r, c = lax.axis_index("radial"), lax.axis_index("chan")
    z, x, core = r // 8, lax.rem(r, 8) // 2, lax.rem(r, 2)
    is_root = r == 0
    self_plane = c == z
    up, down = lax.rem(r + 1, NRAD), lax.rem(r + NRAD - 1, NRAD)

    is_first, is_second = core == 0, core == 1

    zero_rows = jnp.zeros((4, 64, 1920), BF16)
    stage[:, 0:64, :] = zero_rows
    stage[:, ROWS:RP, :] = zero_rows

    def ham_copy(i):
        return pltpu.make_async_copy(
            ham_hbm.at[:, pl.ds(1920 * i, 1920)],
            stage.at[i, pl.ds(pl.multiple_of(64 * core, 64), ROWS)],
            ham_sem.at[i],
        )

    for i in range(4):
        ham_copy(i).start()

    barrier = pltpu.get_barrier_semaphore()

    def greet(device):
        pl.semaphore_signal(barrier, inc=1, device_id=device, device_id_type=MESH)

    for i in range(8):
        producer = 8 * c + i

        @pl.when(producer != r)
        def _():
            greet((producer, c))

    for d in range(1, NCH):
        greet((r, lax.rem(c + d, NCH)))
    greet((up, c))
    greet((down, c))

    @pl.when(is_root)
    def _():
        for d in range(1, NRAD):
            greet((d, c))

    @pl.when(jnp.logical_not(is_root))
    def _():
        greet((0, c))

    opad[:, 256:CP, :] = jnp.zeros((2, CP - 256, PTS), F32)
    for s in range(2):
        opad[s, 0:LC, :] = outer[:, s, :]
    for s in range(2):
        for cb in range(3):
            for pb in range(2):
                ut[s, HALO + 128 * pb : HALO + 128 * (pb + 1), 128 * cb : 128 * (cb + 1)] = opad[
                    s, 128 * cb : 128 * (cb + 1), 128 * pb : 128 * (pb + 1)
                ].T
    surf[...] = jnp.zeros_like(surf)
    v0p[...] = jnp.zeros_like(v0p)

    def place_rows(at):
        for m in range(2):
            surf[m, 0:LC, at : at + ROWS] = surf_in[:, m, :]
        v0p[0:2, at : at + ROWS] = v0[...]

    pl.when(is_first)(lambda: place_rows(0))
    pl.when(is_second)(lambda: place_rows(RP - ROWS))

    u[:, :, 0:8, :] = jnp.zeros((NCH, 2, 8, CP), F32)
    u[:, :, 104:112, :] = jnp.zeros((NCH, 2, 8, CP), F32)
    for i in range(NCH):
        call[CP * i + CR : CP * (i + 1), :] = jnp.zeros((CP - CR, NCH * CP), BF16)
    total[...] = jnp.zeros_like(total)

    dpad[...] = jnp.zeros_like(dpad)
    dpad[0:LC, 0 : NCH * LC] = dipole[...]
    pads[...] = jnp.full(pads.shape, -1, jnp.int32)
    pads[0:1, 0 : NCH * LC] = target[...].reshape(1, NCH * LC)
    pads[1:2, 0 : NCH * LC] = mom[...].reshape(1, NCH * LC)
    kind = row_iota((64, 1280))
    features = jnp.where(
        kind < 32, (kind == pads[0:1, :]).astype(F32), (kind - 32 == pads[1:2, :]).astype(F32)
    ).astype(BF16)
    row64, col64 = row_iota((64, 64)), lax.broadcasted_iota(jnp.int32, (64, 64), 1)
    m64[...] = jnp.where(jnp.logical_and(row64 >= 32, jnp.abs(row64 - col64) == 1), jnp.where(col64 >= 32, 1.0, 0.0), 0.0)
    m64[0:8, 0:8] = couple_mask[...].astype(F32)
    moments = jnp.where(row_iota((8, 64)) == 0, lax.broadcasted_iota(jnp.int32, (8, 64), 1) - 32, 0)
    moments = jnp.where(lax.broadcasted_iota(jnp.int32, (8, 64), 1) >= 32, moments, 0).astype(F32).astype(BF16)

    def selection(i):
        at = row_iota((512, CP)) + 256 * i - LC * i
        column = lax.broadcasted_iota(jnp.int32, (512, CP), 1)
        return jnp.where(jnp.logical_and(at == column, column < LC), 1.0, 0.0).astype(BF16)

    for i in range(NCH):
        hot[i] = nn_dot(features[:, 256 * i : 256 * i + 512], selection(i))
        lval = nn_dot(moments, hot[i].astype(BF16))[0:1]
        lmom[i : i + 1, :] = lval * (lval + 1.0) * 0.5
    mine = hot[c].T.astype(BF16)
    for i in range(NCH):
        met = nn_dot(mine, nn_dot(m64[...].astype(BF16), hot[i].astype(BF16)).astype(BF16))
        moved = nn_dot(dpad[:, 256 * i : 256 * i + 512], selection(i))
        cloc[:, CP * i : CP * (i + 1)] = jnp.where(met > 1.5, moved, 0.0).astype(BF16)

    call[pl.ds(pl.multiple_of(CP * c, CP), CP), :] = cloc[...]

    def take_matrix(i):
        ham_copy(i).wait()

        def turn(j, _):
            at = pl.ds(pl.multiple_of(128 * j, 128), 128)
            hamt[i, at, :] = stage[i, :, at].T
            return 0

        lax.fori_loop(0, 15, turn, 0)

    for i in range(2):
        take_matrix(i)

    greeted = 5 + jnp.where(self_plane, NRAD - 1, 0) + jnp.where(is_root, NRAD - 1, 1)
    pl.semaphore_wait(barrier, greeted)

    def send_term(k, lo, hi):
        ps, slot = lax.rem(k, 2), lax.rem(k, SLOTS)

        @pl.when(k >= 3)
        def _():
            bytes_wait(yrec.at[0, pl.ds(0, 3)], ys_sem.at[ps])

        both = jnp.concatenate([lo, hi], axis=0)
        ysend[ps] = both
        yrec[slot, c] = both
        for d in (2, 1, 3):
            pltpu.make_async_remote_copy(
                src_ref=ysend.at[ps],
                dst_ref=yrec.at[slot, c],
                send_sem=ys_sem.at[ps],
                recv_sem=yr_sem.at[slot],
                device_id=(r, lax.rem(c + d, NCH)),
                device_id_type=MESH,
            ).start()

    def spread(k):
        ps, slot = lax.rem(k, 2), lax.rem(k + SLOTS - 1, SLOTS)

        @pl.when(k >= 3)
        def _():
            bytes_wait(vrec.at[0, pl.ds(0, 31)], vs_sem.at[ps])

        vsend[ps] = term[...].astype(BF16)
        place = vrec.at[slot, 2 * x + core]
        for dz in (2, 1, 3, 0):
            for dx in (2, 1, 3, 0):
                for dc in (1, 0):
                    if dz or dx or dc:
                        rr = 8 * lax.rem(z + dz, 4) + 2 * lax.rem(x + dx, 4) + lax.rem(core + dc, 2)
                        pltpu.make_async_remote_copy(
                            src_ref=vsend.at[ps],
                            dst_ref=place,
                            send_sem=vs_sem.at[ps],
                            recv_sem=vr_sem.at[slot, x],
                            device_id=(rr, c),
                            device_id_type=MESH,
                        ).start()
        pltpu.make_async_copy(vsend.at[ps], place, vr_sem.at[slot, x]).start()

    def send_edge(k, rows):
        slot = lax.rem(k, SLOTS)
        for i in range(4):
            erec[slot, i : i + 1, :] = rows[i]
        for d in range(1, NRAD):
            pltpu.make_async_remote_copy(
                src_ref=erec.at[slot],
                dst_ref=erec.at[slot],
                send_sem=es_sem.at[slot],
                recv_sem=er_sem.at[slot],
                device_id=((d * 11) % NRAD, c),
                device_id_type=MESH,
            ).start()

    def send_strip(k):
        slot = lax.rem(k, SLOTS)
        for s in range(2):
            strec[slot, c, STRIP * s : STRIP * (s + 1), :] = strip[s, 8 : 8 + STRIP, :].astype(BF16)
        for d in (2, 1, 3):
            pltpu.make_async_remote_copy(
                src_ref=strec.at[slot, c],
                dst_ref=strec.at[slot, c],
                send_sem=ss_sem.at[slot],
                recv_sem=sr_sem.at[slot],
                device_id=(0, lax.rem(c + d, NCH)),
                device_id_type=MESH,
            ).start()

    lo, hi = pack(v0p[...])
    term[...] = jnp.concatenate([lo, hi], axis=0)
    itot[...] = term[...]

    @pl.when(is_root)
    def _():
        strip[...] = jnp.zeros_like(strip)
        for s in range(2):
            strip[s, 8 : 8 + STRIP, :] = ut[s, HALO : HALO + STRIP, :]
        stot[...] = jnp.zeros_like(stot)
        send_edge(0, [strip[s, 8 + m : 9 + m, :] for m in range(2) for s in range(2)])
        send_strip(0)

    def halo_copies():
        low = pltpu.make_async_remote_copy(
            src_ref=ut.at[:, pl.ds(HALO, HALO)], dst_ref=ut.at[:, pl.ds(HALO + PTS, HALO)],
            send_sem=hs_sem.at[0], recv_sem=hr_sem.at[0], device_id=(down, c), device_id_type=MESH,
        )
        high = pltpu.make_async_remote_copy(
            src_ref=ut.at[:, pl.ds(PTS, HALO)], dst_ref=ut.at[:, pl.ds(0, HALO)],
            send_sem=hs_sem.at[1], recv_sem=hr_sem.at[1], device_id=(up, c), device_id_type=MESH,
        )
        return low, high

    for cp in halo_copies():
        cp.start()

    def block_copy(d):
        cc = lax.rem(c + d, NCH)
        return pltpu.make_async_remote_copy(
            src_ref=ut.at[:, pl.ds(pl.multiple_of(BLK * cc, BLK), BLK + 2 * HALO)],
            dst_ref=u.at[c, :, pl.ds(8, BLK + 2 * HALO)],
            send_sem=us_sem.at[d - 1], recv_sem=ur_sem.at[d - 1],
            device_id=(r, cc), device_id_type=MESH,
        )

    def half(i):
        return pl.ds(pl.multiple_of(CP * i + CR // 2 * core, 32), CR // 2)

    def next_block(p, d):
        return lax.rem(p + (2 if d == 1 else 1), NCH)

    def columns(i):
        return pl.ds(pl.multiple_of(CP * i, CP), CP)

    def coupling_copies(d):
        out = []
        for j in range(2):
            cols = columns(c if j == 0 else next_block(c, d))
            out.append(
                pltpu.make_async_remote_copy(
                    src_ref=cloc.at[half(0), cols],
                    dst_ref=call.at[half(c), cols],
                    send_sem=cs_sem.at[2 * d - 2 + j], recv_sem=cr_sem.at[2 * d - 2 + j],
                    device_id=(r, lax.rem(c + d, NCH)), device_id_type=MESH,
                )
            )
        return out

    def share_copies(d):
        p = lax.rem(c + NCH - d, NCH)
        out = []
        for j in range(2):
            place = call.at[half(p), columns(p if j == 0 else next_block(p, d))]
            out.append(
                pltpu.make_async_remote_copy(
                    src_ref=place, dst_ref=place,
                    send_sem=ds_sem.at[2 * d - 2 + j], recv_sem=dr_sem.at[2 * d - 2 + j],
                    device_id=(r + 1 - 2 * core, c), device_id_type=MESH,
                )
            )
        return out

    def mirror(a, b):
        call[columns(b), columns(a)] = call[columns(a), columns(b)].T

    def final_copy(d):
        cc = lax.rem(c + d, NCH)
        return pltpu.make_async_remote_copy(
            src_ref=total.at[cc], dst_ref=fin.at[c],
            send_sem=fs_sem.at[d - 1], recv_sem=fr_sem.at[d - 1],
            device_id=(r, cc), device_id_type=MESH,
        )

    def own_block():
        return ut[:, pl.ds(pl.multiple_of(BLK * c, BLK), BLK + 2 * HALO), :]

    def outer_step(k):
        f = time_step / lax.convert_element_type(k, F32)
        for cp in range(NCH):
            for s in range(2):
                uh[96 * s : 96 * (s + 1), CP * cp : CP * (cp + 1)] = u[cp, s, 8:104, :].astype(BF16)
        for h in range(2):
            mix[:, 768 * h : 768 * (h + 1)] = nn_dot(uh[...], call[:, 768 * h : 768 * (h + 1)])
        point = PTS * r + BLK * c - HALO + row_iota((96, 1))
        valid = jnp.logical_and(point >= 0, point < NRAD * PTS)
        radius = inner_radius + grid_step * (point.astype(F32) + 1.0)
        inv = 1.0 / (radius * radius)

        def chunk(cc, _):
            applied = []
            for s in range(2):
                w = u[cc, s, 8:104, :]
                lap = (
                    (u[cc, s, 6:102, :] + u[cc, s, 10:106, :])
                    - 16.0 * (u[cc, s, 7:103, :] + u[cc, s, 9:105, :])
                    + 30.0 * w
                )
                applied.append(
                    lap_gain * lap + (lmom[pl.ds(cc, 1), :] * inv) * w + radius * mix[96 * s : 96 * (s + 1), columns(cc)]
                )
            new = (jnp.where(valid, f * applied[1], 0.0), jnp.where(valid, -f * applied[0], 0.0))
            for s in range(2):
                u[cc, s, 8:104, :] = new[s]
                total[cc, s] += new[s][HALO : HALO + BLK]
            return 0

        lax.fori_loop(0, NCH, chunk, 0)

    first = 4

    def outer_when(k, start, index):
        @pl.when(jnp.logical_and(k >= start, k < start + 4))
        def _():
            outer_step(index)

    def step(k, _):
        ps, slot, before = lax.rem(k, 2), lax.rem(k, SLOTS), lax.rem(k + SLOTS - 1, SLOTS)
        f = time_step / lax.convert_element_type(k, F32)

        @pl.when(self_plane)
        def _():
            spread(k)

        rows = jnp.concatenate(unpack(term[0:8], term[8:16]), axis=1).astype(BF16)
        g0, g1 = nt_dot(rows, surf[0]), nt_dot(rows, surf[1])
        ghost = jnp.where(row_iota((8, CP)) < 2, g0, pltpu.roll(g1, 2, 0))[0:4]

        @pl.when(is_root)
        def _():
            grec[slot, 0] = ghost

        @pl.when(jnp.logical_not(is_root))
        def _():
            @pl.when(k >= 3)
            def _():
                bytes_wait(grec.at[0, 0], gs_sem.at[ps])

            gsend[ps] = ghost
            pltpu.make_async_remote_copy(
                src_ref=gsend.at[ps], dst_ref=grec.at[slot, r],
                send_sem=gs_sem.at[ps], recv_sem=gr_sem.at[slot],
                device_id=(0, c), device_id_type=MESH,
            ).start()

        @pl.when(k == 1)
        def _():
            for d in (2, 1, 3):
                for cp in coupling_copies(d):
                    cp.start()
            take_matrix(2)

        @pl.when(k == 1)
        def _():
            for cp in halo_copies():
                cp.wait()

            @pl.when(r == NRAD - 1)
            def _():
                ut[:, HALO + PTS :, :] = jnp.zeros((2, HALO, CP), F32)

            for d in (2, 1, 3):
                block_copy(d).start()
            u[c, :, 8:104, :] = own_block()
            take_matrix(3)

        @pl.when(k == first - 1)
        def _():
            for d in (2, 1, 3):
                for cp in coupling_copies(d):
                    cp.wait()
                for cp in share_copies(d):
                    cp.start()

        def take_coupling():
            for d in (2, 1, 3):
                for cp in share_copies(d):
                    cp.wait()
            for d in (1, 2, 3):
                mirror(c, lax.rem(c + d, NCH))
                p = lax.rem(c + NCH - d, NCH)
                mirror(p, next_block(p, d))
                block_copy(d).wait()

        outer_when(k, first, 2 * (k - first) + 1)

        acc = jnp.zeros((8, RP), F32)
        for off in (0, 1, 3, 2):
            if off == 2:
                @pl.when(jnp.logical_not(is_root))
                def _():
                    bytes_wait(erec.at[before], er_sem.at[before])

                edge = jnp.concatenate([erec[before], jnp.zeros((4, CP), F32)], axis=0).astype(BF16)
                acc += surface_gain * (nn_dot(edge, surf[0]) + pltpu.roll(nn_dot(edge, surf[1]), 6, 0))

            xi = lax.rem(x + off, 4)
            bytes_wait(vrec.at[before, pl.ds(2 * xi, 2)], vr_sem.at[before, xi])
            tiles = []
            for co in range(2):
                both = vrec[before, 2 * xi + co].astype(F32)
                tiles.append(unpack(both[0:8], both[8:16]))
            lanes = tiles[0][:7] + [tiles[0][7] + tiles[1][0]] + tiles[1][1:]
            lhs = jnp.concatenate(lanes, axis=1).astype(BF16)
            acc += nn_dot(lhs, hamt[xi])

        lo, hi = pack(acc)
        send_term(k, times_minus_i(lo, f), times_minus_i(hi, f))

        @pl.when(is_root)
        def _():
            bytes_wait(strec.at[before, pl.ds(0, 3)], sr_sem.at[before])
            mixed = jnp.zeros((2 * STRIP, CP), F32)
            for cp in range(NCH):
                mixed += nt_dot(strec[before, cp], cloc[:, CP * cp : CP * (cp + 1)])
            bytes_wait(grec.at[slot, pl.ds(0, NRAD - 1)], gr_sem.at[slot])
            seen = jnp.zeros((4, CP), F32)
            for i in range(NRAD):
                seen += grec[slot, i]
            for s in range(2):
                strip[s, 7:8, :] = seen[s : s + 1]
                strip[s, 6:7, :] = seen[2 + s : 3 + s]
            radius = inner_radius + grid_step * (row_iota((STRIP, 1)).astype(F32) + 1.0)
            inv = 1.0 / (radius * radius)
            applied = []
            for s in range(2):
                w = strip[s, 8 : 8 + STRIP, :]
                lap = (
                    (strip[s, 6 : 6 + STRIP, :] + strip[s, 10 : 10 + STRIP, :])
                    - 16.0 * (strip[s, 7 : 7 + STRIP, :] + strip[s, 9 : 9 + STRIP, :])
                    + 30.0 * w
                )
                applied.append(
                    lap_gain * lap + (lmom[pl.ds(c, 1), :] * inv) * w + radius * mixed[STRIP * s : STRIP * (s + 1)]
                )
            new = (f * applied[1], -f * applied[0])
            for s in range(2):
                strip[s, 8 : 8 + STRIP, :] = new[s]
                stot[s] += new[s]
            bytes_wait(strec.at[0, pl.ds(0, 3)], ss_sem.at[before])
            bytes_wait(grec.at[0, pl.ds(0, NRAD - 1)], es_sem.at[before])

            @pl.when(k < ORDER)
            def _():
                send_edge(k, [new[s][m : m + 1] for m in range(2) for s in range(2)])
                send_strip(k)

        pl.when(k == first - 1)(take_coupling)
        outer_when(k, first, 2 * (k - first) + 2)

        @pl.when(k == first + 3)
        def _():
            for d in (2, 1, 3):
                final_copy(d).start()
            fin[c] = total[c]

        bytes_wait(yrec.at[slot, pl.ds(0, 3)], yr_sem.at[slot])
        own = (yrec[slot, 0] + yrec[slot, 1]) + (yrec[slot, 2] + yrec[slot, 3])
        itot[...] += own
        term[...] = own
        return 0

    lax.fori_loop(1, ORDER + 1, step, 0)

    inner = jnp.concatenate(unpack(itot[0:8], itot[8:16]), axis=1)[0:2]

    @pl.when(is_first)
    def _():
        inner_ref[...] = inner[:, 0:ROWS]

    @pl.when(is_second)
    def _():
        inner_ref[...] = inner[:, RP - ROWS : RP]

    for d in (1, 2, 3):
        final_copy(d).wait()

    @pl.when(is_root)
    def _():
        for s in range(2):
            fin[0, s, 0:HALO, :] = stot[s, 0:HALO, :]

    for s in range(2):
        for pb in range(2):
            rows = jnp.concatenate([fin[2 * pb, s], fin[2 * pb + 1, s]], axis=0)
            for cb in range(3):
                n = min(128, LC - 128 * cb)
                out_ref[128 * cb : 128 * cb + n, s, 128 * pb : 128 * (pb + 1)] = (
                    opad[s, 128 * cb : 128 * cb + n, 128 * pb : 128 * (pb + 1)]
                    + rows[:, 128 * cb : 128 * (cb + 1)].T[0:n]
                )

    for k in (ORDER - 1, ORDER):
        bytes_wait(yrec.at[0, pl.ds(0, 3)], ys_sem.at[k % 2])

        @pl.when(self_plane)
        def _():
            bytes_wait(vrec.at[0, pl.ds(0, 31)], vs_sem.at[k % 2])

        @pl.when(jnp.logical_not(is_root))
        def _():
            bytes_wait(grec.at[0, 0], gs_sem.at[k % 2])


def hand_on(out, inner, out_ref, inner_ref):
    out_ref[...] = out[...]
    inner_ref[...] = inner[...]


def local(outer_wave, inner_wave, inner_ham, surface, dipole, ang_mom, target, couple_mask):
    vm = pl.BlockSpec(memory_space=pltpu.VMEM)
    dma = pltpu.SemaphoreType.DMA
    out, inner = pl.pallas_call(
        kernel,
        out_shape=(
            jax.ShapeDtypeStruct((LC, 2, PTS), F32),
            jax.ShapeDtypeStruct((2, ROWS), F32),
        ),
        in_specs=[pl.BlockSpec(memory_space=pl.ANY)] + [vm] * 7,
        out_specs=(vm, vm),
        scratch_shapes=[
            pltpu.VMEM((2, CP, RP), BF16),
            pltpu.VMEM((CP, NCH * CP), BF16),
            pltpu.VMEM((CP, 1280), BF16),
            pltpu.VMEM((8, 1280), jnp.int32),
            pltpu.VMEM((NCH, 64, CP), F32),
            pltpu.VMEM((NCH, CP), F32),
            pltpu.VMEM((64, 64), F32),
            pltpu.VMEM((8, RP), F32),
            pltpu.VMEM((4, RP, 1920), BF16),
            pltpu.VMEM((4, 1920, RP), BF16),
            pltpu.VMEM((2, CP, PTS), F32),
            pltpu.VMEM((2, PTS + 2 * HALO, CP), F32),
            pltpu.VMEM((NCH, 2, 112, CP), F32),
            pltpu.VMEM((192, NCH * CP), BF16),
            pltpu.VMEM((192, NCH * CP), F32),
            pltpu.VMEM((NCH * CP, NCH * CP), BF16),
            pltpu.VMEM((NCH, 2, BLK, CP), F32),
            pltpu.VMEM((NCH, 2, BLK, CP), F32),
            pltpu.VMEM((2, 16, 128), BF16),
            pltpu.VMEM((SLOTS, 32, 16, 128), BF16),
            pltpu.VMEM((2, 16, 128), F32),
            pltpu.VMEM((SLOTS, NCH, 16, 128), F32),
            pltpu.VMEM((16, 128), F32),
            pltpu.VMEM((16, 128), F32),
            pltpu.VMEM((2, 4, CP), F32),
            pltpu.VMEM((SLOTS, NRAD, 4, CP), F32),
            pltpu.VMEM((SLOTS, 4, CP), F32),
            pltpu.VMEM((2, 48, CP), F32),
            pltpu.VMEM((2, STRIP, CP), F32),
            pltpu.VMEM((SLOTS, NCH, 2 * STRIP, CP), BF16),
            dma((4,)),
            dma((2,)), dma((SLOTS, 4)),
            dma((2,)), dma((SLOTS,)),
            dma((2,)), dma((SLOTS,)),
            dma((SLOTS,)), dma((SLOTS,)),
            dma((SLOTS,)), dma((SLOTS,)),
            dma((2,)), dma((2,)),
            dma((3,)), dma((3,)),
            dma((6,)), dma((6,)),
            dma((6,)), dma((6,)),
            dma((3,)), dma((3,)),
        ],
        compiler_params=pltpu.CompilerParams(
            collective_id=0, has_side_effects=True, vmem_limit_bytes=58 * 2**20
        ),
    )(
        inner_ham,
        jnp.transpose(surface, (1, 0, 2)),
        dipole,
        jnp.transpose(outer_wave, (1, 0, 2)),
        inner_wave,
        ang_mom,
        target,
        couple_mask,
    )
    out, inner = pl.pallas_call(
        hand_on,
        out_shape=(jax.ShapeDtypeStruct(out.shape, F32), jax.ShapeDtypeStruct(inner.shape, F32)),
        in_specs=[vm, vm],
        out_specs=(vm, vm),
    )(out, inner)
    return jnp.transpose(out, (1, 0, 2)), inner


def solution(mesh):
    placed = (
        P(None, "chan", "radial"),
        P(None, "radial"),
        P("radial", "chan"),
        P(None, "chan", "radial"),
        P("chan", None),
        P(),
        P(),
        P(),
    )
    return jax.shard_map(
        local,
        mesh=mesh,
        in_specs=placed,
        out_specs=(P(None, "chan", "radial"), P(None, "radial")),
        check_vma=False,
    )
```

```python
import jax
import jax.numpy as jnp
from jax import lax
from jax.experimental import pallas as pl
from jax.experimental.pallas import tpu as pltpu
from jax.sharding import PartitionSpec as P

ORDER = 8
time_step = 0.008
grid_step = 0.08
inner_radius = 20.0
surface_gain = 16.0 / (24.0 * grid_step * grid_step)
lap_gain = 1.0 / (24.0 * grid_step * grid_step)

MESH = pl.DeviceIdType.MESH
F32, BF16 = jnp.float32, jnp.bfloat16
NRAD, NCH = 32, 4
ROWS, LC, PTS = 960, 300, 256
RP, CP = 1024, 384
SLOTS = 4
HALO, BLK = 16, 64
CR = 320
STRIP = 32
NT = (((1,), (1,)), ((), ()))


def nt_dot(a, b):
    return lax.dot_general(a, b, NT, preferred_element_type=F32)


def nn_dot(a, b):
    return jnp.dot(a, b, preferred_element_type=F32)


def bytes_wait(ref, sem):
    pltpu.make_async_copy(ref, ref, sem).wait()


def row_iota(shape):
    return lax.broadcasted_iota(jnp.int32, shape, 0)


def pack(a):
    row = row_iota((8, 128))
    halves = []
    for h in range(2):
        t = a[:, 512 * h : 512 * h + 128]
        for q in range(1, 4):
            piece = a[:, 512 * h + 128 * q : 512 * h + 128 * (q + 1)]
            t = jnp.where(row // 2 == q, pltpu.roll(piece, 2 * q, 0), t)
        halves.append(t)
    return halves


def unpack(lo, hi):
    out = []
    for h in (lo, hi):
        for q in range(4):
            out.append(h if q == 0 else pltpu.roll(h, 8 - 2 * q, 0))
    return out


def times_minus_i(t, f):
    even = row_iota((8, 128)) % 2 == 0
    return jnp.where(even, f * pltpu.roll(t, 7, 0), -f * pltpu.roll(t, 1, 0))


def kernel(
    ham_hbm, surf_in, dipole, outer, v0, mom, target, couple_mask,
    out_ref, inner_ref,
    surf, cloc, dpad, pads, hot, lmom, m64, v0p, stage, hamt, opad, ut, u, uh, mix, call, total, fin,
    vsend, vrec, ysend, yrec, itot, term, gsend, grec, erec, strip, stot, strec,
    ham_sem, vs_sem, vr_sem, ys_sem, yr_sem, gs_sem, gr_sem, es_sem, er_sem, ss_sem, sr_sem,
    hs_sem, hr_sem, us_sem, ur_sem, cs_sem, cr_sem, ds_sem, dr_sem, fs_sem, fr_sem,
):
    r, c = lax.axis_index("radial"), lax.axis_index("chan")
    z, x, core = r // 8, lax.rem(r, 8) // 2, lax.rem(r, 2)
    is_root = r == 0
    self_plane = c == z
    up, down = lax.rem(r + 1, NRAD), lax.rem(r + NRAD - 1, NRAD)

    is_first, is_second = core == 0, core == 1

    zero_rows = jnp.zeros((4, 64, 1920), BF16)
    stage[:, 0:64, :] = zero_rows
    stage[:, ROWS:RP, :] = zero_rows

    def ham_copy(i):
        return pltpu.make_async_copy(
            ham_hbm.at[:, pl.ds(1920 * i, 1920)],
            stage.at[i, pl.ds(pl.multiple_of(64 * core, 64), ROWS)],
            ham_sem.at[i],
        )

    for i in range(4):
        ham_copy(i).start()

    barrier = pltpu.get_barrier_semaphore()

    def greet(device):
        pl.semaphore_signal(barrier, inc=1, device_id=device, device_id_type=MESH)

    for i in range(8):
        producer = 8 * c + i

        @pl.when(producer != r)
        def _():
            greet((producer, c))

    for d in range(1, NCH):
        greet((r, lax.rem(c + d, NCH)))
    greet((up, c))
    greet((down, c))

    @pl.when(is_root)
    def _():
        for d in range(1, NRAD):
            greet((d, c))

    @pl.when(jnp.logical_not(is_root))
    def _():
        greet((0, c))

    opad[:, 256:CP, :] = jnp.zeros((2, CP - 256, PTS), F32)
    for s in range(2):
        opad[s, 0:LC, :] = outer[:, s, :]
    for s in range(2):
        for cb in range(3):
            for pb in range(2):
                ut[s, HALO + 128 * pb : HALO + 128 * (pb + 1), 128 * cb : 128 * (cb + 1)] = opad[
                    s, 128 * cb : 128 * (cb + 1), 128 * pb : 128 * (pb + 1)
                ].T
    surf[...] = jnp.zeros_like(surf)
    v0p[...] = jnp.zeros_like(v0p)

    def place_rows(at):
        for m in range(2):
            surf[m, 0:LC, at : at + ROWS] = surf_in[:, m, :]
        v0p[0:2, at : at + ROWS] = v0[...]

    pl.when(is_first)(lambda: place_rows(0))
    pl.when(is_second)(lambda: place_rows(RP - ROWS))

    u[:, :, 0:8, :] = jnp.zeros((NCH, 2, 8, CP), F32)
    u[:, :, 104:112, :] = jnp.zeros((NCH, 2, 8, CP), F32)
    for i in range(NCH):
        call[CP * i + CR : CP * (i + 1), :] = jnp.zeros((CP - CR, NCH * CP), BF16)
    total[...] = jnp.zeros_like(total)

    dpad[...] = jnp.zeros_like(dpad)
    dpad[0:LC, 0 : NCH * LC] = dipole[...]
    pads[...] = jnp.full(pads.shape, -1, jnp.int32)
    pads[0:1, 0 : NCH * LC] = target[...].reshape(1, NCH * LC)
    pads[1:2, 0 : NCH * LC] = mom[...].reshape(1, NCH * LC)
    kind = row_iota((64, 1280))
    features = jnp.where(
        kind < 32, (kind == pads[0:1, :]).astype(F32), (kind - 32 == pads[1:2, :]).astype(F32)
    ).astype(BF16)
    row64, col64 = row_iota((64, 64)), lax.broadcasted_iota(jnp.int32, (64, 64), 1)
    m64[...] = jnp.where(jnp.logical_and(row64 >= 32, jnp.abs(row64 - col64) == 1), jnp.where(col64 >= 32, 1.0, 0.0), 0.0)
    m64[0:8, 0:8] = couple_mask[...].astype(F32)
    moments = jnp.where(row_iota((8, 64)) == 0, lax.broadcasted_iota(jnp.int32, (8, 64), 1) - 32, 0)
    moments = jnp.where(lax.broadcasted_iota(jnp.int32, (8, 64), 1) >= 32, moments, 0).astype(F32).astype(BF16)

    def selection(i):
        at = row_iota((512, CP)) + 256 * i - LC * i
        column = lax.broadcasted_iota(jnp.int32, (512, CP), 1)
        return jnp.where(jnp.logical_and(at == column, column < LC), 1.0, 0.0).astype(BF16)

    for i in range(NCH):
        hot[i] = nn_dot(features[:, 256 * i : 256 * i + 512], selection(i))
        lval = nn_dot(moments, hot[i].astype(BF16))[0:1]
        lmom[i : i + 1, :] = lval * (lval + 1.0) * 0.5
    mine = hot[c].T.astype(BF16)
    for i in range(NCH):
        met = nn_dot(mine, nn_dot(m64[...].astype(BF16), hot[i].astype(BF16)).astype(BF16))
        moved = nn_dot(dpad[:, 256 * i : 256 * i + 512], selection(i))
        cloc[:, CP * i : CP * (i + 1)] = jnp.where(met > 1.5, moved, 0.0).astype(BF16)

    call[pl.ds(pl.multiple_of(CP * c, CP), CP), :] = cloc[...]

    def take_matrix(i):
        ham_copy(i).wait()

        def turn(j, _):
            at = pl.ds(pl.multiple_of(128 * j, 128), 128)
            hamt[i, at, :] = stage[i, :, at].T
            return 0

        lax.fori_loop(0, 15, turn, 0)

    for i in range(2):
        take_matrix(i)

    greeted = 5 + jnp.where(self_plane, NRAD - 1, 0) + jnp.where(is_root, NRAD - 1, 1)
    pl.semaphore_wait(barrier, greeted)

    def send_term(k, lo, hi):
        ps, slot = lax.rem(k, 2), lax.rem(k, SLOTS)

        @pl.when(k >= 3)
        def _():
            bytes_wait(yrec.at[0, pl.ds(0, 3)], ys_sem.at[ps])

        both = jnp.concatenate([lo, hi], axis=0)
        ysend[ps] = both
        yrec[slot, c] = both
        for d in (2, 1, 3):
            pltpu.make_async_remote_copy(
                src_ref=ysend.at[ps],
                dst_ref=yrec.at[slot, c],
                send_sem=ys_sem.at[ps],
                recv_sem=yr_sem.at[slot],
                device_id=(r, lax.rem(c + d, NCH)),
                device_id_type=MESH,
            ).start()

    def spread(k):
        ps, slot = lax.rem(k, 2), lax.rem(k + SLOTS - 1, SLOTS)

        @pl.when(k >= 3)
        def _():
            bytes_wait(vrec.at[0, pl.ds(0, 31)], vs_sem.at[ps])

        vsend[ps] = term[...].astype(BF16)
        place = vrec.at[slot, 2 * x + core]
        for dz in (2, 1, 3, 0):
            for dx in (2, 1, 3, 0):
                for dc in (1, 0):
                    if dz or dx or dc:
                        rr = 8 * lax.rem(z + dz, 4) + 2 * lax.rem(x + dx, 4) + lax.rem(core + dc, 2)
                        pltpu.make_async_remote_copy(
                            src_ref=vsend.at[ps],
                            dst_ref=place,
                            send_sem=vs_sem.at[ps],
                            recv_sem=vr_sem.at[slot, x],
                            device_id=(rr, c),
                            device_id_type=MESH,
                        ).start()
        pltpu.make_async_copy(vsend.at[ps], place, vr_sem.at[slot, x]).start()

    def send_edge(k, rows):
        slot = lax.rem(k, SLOTS)
        for i in range(4):
            erec[slot, i : i + 1, :] = rows[i]
        for d in range(1, NRAD):
            pltpu.make_async_remote_copy(
                src_ref=erec.at[slot],
                dst_ref=erec.at[slot],
                send_sem=es_sem.at[slot],
                recv_sem=er_sem.at[slot],
                device_id=((d * 11) % NRAD, c),
                device_id_type=MESH,
            ).start()

    def send_strip(k):
        slot = lax.rem(k, SLOTS)
        for s in range(2):
            strec[slot, c, STRIP * s : STRIP * (s + 1), :] = strip[s, 8 : 8 + STRIP, :].astype(BF16)
        for d in (2, 1, 3):
            pltpu.make_async_remote_copy(
                src_ref=strec.at[slot, c],
                dst_ref=strec.at[slot, c],
                send_sem=ss_sem.at[slot],
                recv_sem=sr_sem.at[slot],
                device_id=(0, lax.rem(c + d, NCH)),
                device_id_type=MESH,
            ).start()

    lo, hi = pack(v0p[...])
    term[...] = jnp.concatenate([lo, hi], axis=0)
    itot[...] = term[...]

    @pl.when(is_root)
    def _():
        strip[...] = jnp.zeros_like(strip)
        for s in range(2):
            strip[s, 8 : 8 + STRIP, :] = ut[s, HALO : HALO + STRIP, :]
        stot[...] = jnp.zeros_like(stot)
        send_edge(0, [strip[s, 8 + m : 9 + m, :] for m in range(2) for s in range(2)])
        send_strip(0)

    def halo_copies():
        low = pltpu.make_async_remote_copy(
            src_ref=ut.at[:, pl.ds(HALO, HALO)], dst_ref=ut.at[:, pl.ds(HALO + PTS, HALO)],
            send_sem=hs_sem.at[0], recv_sem=hr_sem.at[0], device_id=(down, c), device_id_type=MESH,
        )
        high = pltpu.make_async_remote_copy(
            src_ref=ut.at[:, pl.ds(PTS, HALO)], dst_ref=ut.at[:, pl.ds(0, HALO)],
            send_sem=hs_sem.at[1], recv_sem=hr_sem.at[1], device_id=(up, c), device_id_type=MESH,
        )
        return low, high

    for cp in halo_copies():
        cp.start()

    def block_copy(d, s):
        cc = lax.rem(c + d, NCH)
        return pltpu.make_async_remote_copy(
            src_ref=ut.at[s, pl.ds(pl.multiple_of(BLK * cc, BLK), BLK + 2 * HALO)],
            dst_ref=u.at[c, s, pl.ds(8, BLK + 2 * HALO)],
            send_sem=us_sem.at[2 * d - 2 + s], recv_sem=ur_sem.at[2 * d - 2 + s],
            device_id=(r, cc), device_id_type=MESH,
        )

    def half(i):
        return pl.ds(pl.multiple_of(CP * i + CR // 2 * core, 32), CR // 2)

    def next_block(p, d):
        return lax.rem(p + (2 if d == 1 else 1), NCH)

    def columns(i):
        return pl.ds(pl.multiple_of(CP * i, CP), CP)

    def coupling_copies(d):
        out = []
        for j in range(2):
            cols = columns(c if j == 0 else next_block(c, d))
            out.append(
                pltpu.make_async_remote_copy(
                    src_ref=cloc.at[half(0), cols],
                    dst_ref=call.at[half(c), cols],
                    send_sem=cs_sem.at[2 * d - 2 + j], recv_sem=cr_sem.at[2 * d - 2 + j],
                    device_id=(r, lax.rem(c + d, NCH)), device_id_type=MESH,
                )
            )
        return out

    def share_copies(d):
        p = lax.rem(c + NCH - d, NCH)
        out = []
        for j in range(2):
            place = call.at[half(p), columns(p if j == 0 else next_block(p, d))]
            out.append(
                pltpu.make_async_remote_copy(
                    src_ref=place, dst_ref=place,
                    send_sem=ds_sem.at[2 * d - 2 + j], recv_sem=dr_sem.at[2 * d - 2 + j],
                    device_id=(r + 1 - 2 * core, c), device_id_type=MESH,
                )
            )
        return out

    def mirror(a, b):
        call[columns(b), columns(a)] = call[columns(a), columns(b)].T

    def final_copy(d):
        cc = lax.rem(c + d, NCH)
        return pltpu.make_async_remote_copy(
            src_ref=total.at[cc], dst_ref=fin.at[c],
            send_sem=fs_sem.at[d - 1], recv_sem=fr_sem.at[d - 1],
            device_id=(r, cc), device_id_type=MESH,
        )

    def own_block():
        return ut[:, pl.ds(pl.multiple_of(BLK * c, BLK), BLK + 2 * HALO), :]

    def outer_step(k):
        f = time_step / lax.convert_element_type(k, F32)
        for cp in range(NCH):
            for s in range(2):
                uh[96 * s : 96 * (s + 1), CP * cp : CP * (cp + 1)] = u[cp, s, 8:104, :].astype(BF16)
        for h in range(2):
            mix[:, 768 * h : 768 * (h + 1)] = nn_dot(uh[...], call[:, 768 * h : 768 * (h + 1)])
        point = PTS * r + BLK * c - HALO + row_iota((96, 1))
        valid = jnp.logical_and(point >= 0, point < NRAD * PTS)
        radius = inner_radius + grid_step * (point.astype(F32) + 1.0)
        inv = 1.0 / (radius * radius)

        def chunk(cc, _):
            applied = []
            for s in range(2):
                w = u[cc, s, 8:104, :]
                lap = (
                    (u[cc, s, 6:102, :] + u[cc, s, 10:106, :])
                    - 16.0 * (u[cc, s, 7:103, :] + u[cc, s, 9:105, :])
                    + 30.0 * w
                )
                applied.append(
                    lap_gain * lap + (lmom[pl.ds(cc, 1), :] * inv) * w + radius * mix[96 * s : 96 * (s + 1), columns(cc)]
                )
            new = (jnp.where(valid, f * applied[1], 0.0), jnp.where(valid, -f * applied[0], 0.0))
            for s in range(2):
                u[cc, s, 8:104, :] = new[s]
                total[cc, s] += new[s][HALO : HALO + BLK]
            return 0

        lax.fori_loop(0, NCH, chunk, 0)

    first = 4

    def outer_when(k, start, index):
        @pl.when(jnp.logical_and(k >= start, k < start + 4))
        def _():
            outer_step(index)

    def step(k, _):
        ps, slot, before = lax.rem(k, 2), lax.rem(k, SLOTS), lax.rem(k + SLOTS - 1, SLOTS)
        f = time_step / lax.convert_element_type(k, F32)

        @pl.when(self_plane)
        def _():
            spread(k)

        rows = jnp.concatenate(unpack(term[0:8], term[8:16]), axis=1).astype(BF16)
        g0, g1 = nt_dot(rows, surf[0]), nt_dot(rows, surf[1])
        ghost = jnp.where(row_iota((8, CP)) < 2, g0, pltpu.roll(g1, 2, 0))[0:4]

        @pl.when(is_root)
        def _():
            grec[slot, 0] = ghost

        @pl.when(jnp.logical_not(is_root))
        def _():
            @pl.when(k >= 3)
            def _():
                bytes_wait(grec.at[0, 0], gs_sem.at[ps])

            gsend[ps] = ghost
            pltpu.make_async_remote_copy(
                src_ref=gsend.at[ps], dst_ref=grec.at[slot, r],
                send_sem=gs_sem.at[ps], recv_sem=gr_sem.at[slot],
                device_id=(0, c), device_id_type=MESH,
            ).start()

        @pl.when(k == 1)
        def _():
            for d in (2, 1, 3):
                for cp in coupling_copies(d):
                    cp.start()
            take_matrix(2)

        @pl.when(k == 1)
        def _():
            for cp in halo_copies():
                cp.wait()

            @pl.when(r == NRAD - 1)
            def _():
                ut[:, HALO + PTS :, :] = jnp.zeros((2, HALO, CP), F32)

            u[c, :, 8:104, :] = own_block()
            take_matrix(3)

        @pl.when(k == 2)
        def _():
            for d in (2, 1, 3):
                block_copy(d, 0).start()
            for d in (2, 1, 3):
                for cp in coupling_copies(d):
                    cp.wait()
                for cp in share_copies(d):
                    cp.start()

        @pl.when(k == 3)
        def _():
            for d in (2, 1, 3):
                block_copy(d, 1).start()

        @pl.when(k == first + 4)
        def _():
            for d in (2, 1, 3):
                final_copy(d).start()
            fin[c] = total[c]

        def take_coupling():
            for d in (2, 1, 3):
                for cp in share_copies(d):
                    cp.wait()
            for d in (1, 2, 3):
                mirror(c, lax.rem(c + d, NCH))
                p = lax.rem(c + NCH - d, NCH)
                mirror(p, next_block(p, d))
                block_copy(d, 0).wait()
                block_copy(d, 1).wait()

        outer_when(k, first, 2 * (k - first) + 1)

        acc = jnp.zeros((8, RP), F32)
        for off in (0, 1, 3, 2):
            if off == 2:
                @pl.when(jnp.logical_not(is_root))
                def _():
                    bytes_wait(erec.at[before], er_sem.at[before])

                edge = jnp.concatenate([erec[before], jnp.zeros((4, CP), F32)], axis=0).astype(BF16)
                acc += surface_gain * (nn_dot(edge, surf[0]) + pltpu.roll(nn_dot(edge, surf[1]), 6, 0))

            xi = lax.rem(x + off, 4)
            bytes_wait(vrec.at[before, pl.ds(2 * xi, 2)], vr_sem.at[before, xi])
            tiles = []
            for co in range(2):
                both = vrec[before, 2 * xi + co].astype(F32)
                tiles.append(unpack(both[0:8], both[8:16]))
            lanes = tiles[0][:7] + [tiles[0][7] + tiles[1][0]] + tiles[1][1:]
            lhs = jnp.concatenate(lanes, axis=1).astype(BF16)
            acc += nn_dot(lhs, hamt[xi])

        lo, hi = pack(acc)
        send_term(k, times_minus_i(lo, f), times_minus_i(hi, f))

        @pl.when(is_root)
        def _():
            bytes_wait(strec.at[before, pl.ds(0, 3)], sr_sem.at[before])
            mixed = jnp.zeros((2 * STRIP, CP), F32)
            for cp in range(NCH):
                mixed += nt_dot(strec[before, cp], cloc[:, CP * cp : CP * (cp + 1)])
            bytes_wait(grec.at[slot, pl.ds(0, NRAD - 1)], gr_sem.at[slot])
            seen = jnp.zeros((4, CP), F32)
            for i in range(NRAD):
                seen += grec[slot, i]
            for s in range(2):
                strip[s, 7:8, :] = seen[s : s + 1]
                strip[s, 6:7, :] = seen[2 + s : 3 + s]
            radius = inner_radius + grid_step * (row_iota((STRIP, 1)).astype(F32) + 1.0)
            inv = 1.0 / (radius * radius)
            applied = []
            for s in range(2):
                w = strip[s, 8 : 8 + STRIP, :]
                lap = (
                    (strip[s, 6 : 6 + STRIP, :] + strip[s, 10 : 10 + STRIP, :])
                    - 16.0 * (strip[s, 7 : 7 + STRIP, :] + strip[s, 9 : 9 + STRIP, :])
                    + 30.0 * w
                )
                applied.append(
                    lap_gain * lap + (lmom[pl.ds(c, 1), :] * inv) * w + radius * mixed[STRIP * s : STRIP * (s + 1)]
                )
            new = (f * applied[1], -f * applied[0])
            for s in range(2):
                strip[s, 8 : 8 + STRIP, :] = new[s]
                stot[s] += new[s]
            bytes_wait(strec.at[0, pl.ds(0, 3)], ss_sem.at[before])
            bytes_wait(grec.at[0, pl.ds(0, NRAD - 1)], es_sem.at[before])

            @pl.when(k < ORDER)
            def _():
                send_edge(k, [new[s][m : m + 1] for m in range(2) for s in range(2)])
                send_strip(k)

        pl.when(k == first - 1)(take_coupling)
        outer_when(k, first, 2 * (k - first) + 2)

        bytes_wait(yrec.at[slot, pl.ds(0, 3)], yr_sem.at[slot])
        own = (yrec[slot, 0] + yrec[slot, 1]) + (yrec[slot, 2] + yrec[slot, 3])
        itot[...] += own
        term[...] = own
        return 0

    lax.fori_loop(1, ORDER + 1, step, 0)

    inner = jnp.concatenate(unpack(itot[0:8], itot[8:16]), axis=1)[0:2]

    @pl.when(is_first)
    def _():
        inner_ref[...] = inner[:, 0:ROWS]

    @pl.when(is_second)
    def _():
        inner_ref[...] = inner[:, RP - ROWS : RP]

    for d in (1, 2, 3):
        final_copy(d).wait()

    @pl.when(is_root)
    def _():
        for s in range(2):
            fin[0, s, 0:HALO, :] = stot[s, 0:HALO, :]

    for s in range(2):
        for pb in range(2):
            rows = jnp.concatenate([fin[2 * pb, s], fin[2 * pb + 1, s]], axis=0)
            for cb in range(3):
                n = min(128, LC - 128 * cb)
                out_ref[128 * cb : 128 * cb + n, s, 128 * pb : 128 * (pb + 1)] = (
                    opad[s, 128 * cb : 128 * cb + n, 128 * pb : 128 * (pb + 1)]
                    + rows[:, 128 * cb : 128 * (cb + 1)].T[0:n]
                )

    for k in (ORDER - 1, ORDER):
        bytes_wait(yrec.at[0, pl.ds(0, 3)], ys_sem.at[k % 2])

        @pl.when(self_plane)
        def _():
            bytes_wait(vrec.at[0, pl.ds(0, 31)], vs_sem.at[k % 2])

        @pl.when(jnp.logical_not(is_root))
        def _():
            bytes_wait(grec.at[0, 0], gs_sem.at[k % 2])


def hand_on(out, inner, out_ref, inner_ref):
    out_ref[...] = out[...]
    inner_ref[...] = inner[...]


def local(outer_wave, inner_wave, inner_ham, surface, dipole, ang_mom, target, couple_mask):
    vm = pl.BlockSpec(memory_space=pltpu.VMEM)
    dma = pltpu.SemaphoreType.DMA
    out, inner = pl.pallas_call(
        kernel,
        out_shape=(
            jax.ShapeDtypeStruct((LC, 2, PTS), F32),
            jax.ShapeDtypeStruct((2, ROWS), F32),
        ),
        in_specs=[pl.BlockSpec(memory_space=pl.ANY)] + [vm] * 7,
        out_specs=(vm, vm),
        scratch_shapes=[
            pltpu.VMEM((2, CP, RP), BF16),
            pltpu.VMEM((CP, NCH * CP), BF16),
            pltpu.VMEM((CP, 1280), BF16),
            pltpu.VMEM((8, 1280), jnp.int32),
            pltpu.VMEM((NCH, 64, CP), F32),
            pltpu.VMEM((NCH, CP), F32),
            pltpu.VMEM((64, 64), F32),
            pltpu.VMEM((8, RP), F32),
            pltpu.VMEM((4, RP, 1920), BF16),
            pltpu.VMEM((4, 1920, RP), BF16),
            pltpu.VMEM((2, CP, PTS), F32),
            pltpu.VMEM((2, PTS + 2 * HALO, CP), F32),
            pltpu.VMEM((NCH, 2, 112, CP), F32),
            pltpu.VMEM((192, NCH * CP), BF16),
            pltpu.VMEM((192, NCH * CP), F32),
            pltpu.VMEM((NCH * CP, NCH * CP), BF16),
            pltpu.VMEM((NCH, 2, BLK, CP), F32),
            pltpu.VMEM((NCH, 2, BLK, CP), F32),
            pltpu.VMEM((2, 16, 128), BF16),
            pltpu.VMEM((SLOTS, 32, 16, 128), BF16),
            pltpu.VMEM((2, 16, 128), F32),
            pltpu.VMEM((SLOTS, NCH, 16, 128), F32),
            pltpu.VMEM((16, 128), F32),
            pltpu.VMEM((16, 128), F32),
            pltpu.VMEM((2, 4, CP), F32),
            pltpu.VMEM((SLOTS, NRAD, 4, CP), F32),
            pltpu.VMEM((SLOTS, 4, CP), F32),
            pltpu.VMEM((2, 48, CP), F32),
            pltpu.VMEM((2, STRIP, CP), F32),
            pltpu.VMEM((SLOTS, NCH, 2 * STRIP, CP), BF16),
            dma((4,)),
            dma((2,)), dma((SLOTS, 4)),
            dma((2,)), dma((SLOTS,)),
            dma((2,)), dma((SLOTS,)),
            dma((SLOTS,)), dma((SLOTS,)),
            dma((SLOTS,)), dma((SLOTS,)),
            dma((2,)), dma((2,)),
            dma((6,)), dma((6,)),
            dma((6,)), dma((6,)),
            dma((6,)), dma((6,)),
            dma((3,)), dma((3,)),
        ],
        compiler_params=pltpu.CompilerParams(
            collective_id=0, has_side_effects=True, vmem_limit_bytes=58 * 2**20
        ),
    )(
        inner_ham,
        jnp.transpose(surface, (1, 0, 2)),
        dipole,
        jnp.transpose(outer_wave, (1, 0, 2)),
        inner_wave,
        ang_mom,
        target,
        couple_mask,
    )
    out, inner = pl.pallas_call(
        hand_on,
        out_shape=(jax.ShapeDtypeStruct(out.shape, F32), jax.ShapeDtypeStruct(inner.shape, F32)),
        in_specs=[vm, vm],
        out_specs=(vm, vm),
    )(out, inner)
    return jnp.transpose(out, (1, 0, 2)), inner


def solution(mesh):
    placed = (
        P(None, "chan", "radial"),
        P(None, "radial"),
        P("radial", "chan"),
        P(None, "chan", "radial"),
        P("chan", None),
        P(),
        P(),
        P(),
    )
    return jax.shard_map(
        local,
        mesh=mesh,
        in_specs=placed,
        out_specs=(P(None, "chan", "radial"), P(None, "radial")),
        check_vma=False,
    )
```

```python
import jax
import jax.numpy as jnp
from jax import lax
from jax.experimental import pallas as pl
from jax.experimental.pallas import tpu as pltpu
from jax.sharding import PartitionSpec as P

ORDER = 8
time_step = 0.008
grid_step = 0.08
inner_radius = 20.0
surface_gain = 16.0 / (24.0 * grid_step * grid_step)
lap_gain = 1.0 / (24.0 * grid_step * grid_step)

MESH = pl.DeviceIdType.MESH
F32, BF16 = jnp.float32, jnp.bfloat16
NRAD, NCH = 32, 4
ROWS, LC, PTS = 960, 300, 256
RP, CP = 1024, 384
SLOTS = 4
HALO, BLK = 16, 64
CR = 320
STRIP = 32
NT = (((1,), (1,)), ((), ()))


def nt_dot(a, b):
    return lax.dot_general(a, b, NT, preferred_element_type=F32)


def nn_dot(a, b):
    return jnp.dot(a, b, preferred_element_type=F32)


def bytes_wait(ref, sem):
    pltpu.make_async_copy(ref, ref, sem).wait()


def row_iota(shape):
    return lax.broadcasted_iota(jnp.int32, shape, 0)


def pack(a):
    row = row_iota((8, 128))
    halves = []
    for h in range(2):
        t = a[:, 512 * h : 512 * h + 128]
        for q in range(1, 4):
            piece = a[:, 512 * h + 128 * q : 512 * h + 128 * (q + 1)]
            t = jnp.where(row // 2 == q, pltpu.roll(piece, 2 * q, 0), t)
        halves.append(t)
    return halves


def unpack(lo, hi):
    out = []
    for h in (lo, hi):
        for q in range(4):
            out.append(h if q == 0 else pltpu.roll(h, 8 - 2 * q, 0))
    return out


def times_minus_i(t, f):
    even = row_iota((8, 128)) % 2 == 0
    return jnp.where(even, f * pltpu.roll(t, 7, 0), -f * pltpu.roll(t, 1, 0))


def kernel(
    ham_hbm, surf_in, dipole, outer, v0, mom, target, couple_mask,
    out_ref, inner_ref,
    surf, cloc, dpad, pads, hot, lmom, m64, v0p, stage, hamt, opad, ut, u, uh, mix, call, total, fin,
    vsend, vrec, ysend, yrec, itot, term, gsend, grec, erec, strip, stot, strec,
    ham_sem, vs_sem, vr_sem, ys_sem, yr_sem, gs_sem, gr_sem, es_sem, er_sem, ss_sem, sr_sem,
    hs_sem, hr_sem, us_sem, ur_sem, cs_sem, cr_sem, ds_sem, dr_sem, fs_sem, fr_sem,
):
    r, c = lax.axis_index("radial"), lax.axis_index("chan")
    z, x, core = r // 8, lax.rem(r, 8) // 2, lax.rem(r, 2)
    is_root = r == 0
    self_plane = c == z
    up, down = lax.rem(r + 1, NRAD), lax.rem(r + NRAD - 1, NRAD)

    is_first, is_second = core == 0, core == 1

    zero_rows = jnp.zeros((4, 64, 1920), BF16)
    stage[:, 0:64, :] = zero_rows
    stage[:, ROWS:RP, :] = zero_rows

    def ham_copy(i):
        return pltpu.make_async_copy(
            ham_hbm.at[:, pl.ds(1920 * i, 1920)],
            stage.at[i, pl.ds(pl.multiple_of(64 * core, 64), ROWS)],
            ham_sem.at[i],
        )

    for i in range(4):
        ham_copy(i).start()

    barrier = pltpu.get_barrier_semaphore()

    def greet(device):
        pl.semaphore_signal(barrier, inc=1, device_id=device, device_id_type=MESH)

    for i in range(8):
        producer = 8 * c + i

        @pl.when(producer != r)
        def _():
            greet((producer, c))

    for d in range(1, NCH):
        greet((r, lax.rem(c + d, NCH)))
    greet((up, c))
    greet((down, c))

    @pl.when(is_root)
    def _():
        for d in range(1, NRAD):
            greet((d, c))

    @pl.when(jnp.logical_not(is_root))
    def _():
        greet((0, c))

    opad[:, 256:CP, :] = jnp.zeros((2, CP - 256, PTS), F32)
    for s in range(2):
        opad[s, 0:LC, :] = outer[:, s, :]
    for s in range(2):
        for cb in range(3):
            for pb in range(2):
                ut[s, HALO + 128 * pb : HALO + 128 * (pb + 1), 128 * cb : 128 * (cb + 1)] = opad[
                    s, 128 * cb : 128 * (cb + 1), 128 * pb : 128 * (pb + 1)
                ].T
    surf[...] = jnp.zeros_like(surf)
    v0p[...] = jnp.zeros_like(v0p)

    def place_rows(at):
        for m in range(2):
            surf[m, 0:LC, at : at + ROWS] = surf_in[:, m, :]
        v0p[0:2, at : at + ROWS] = v0[...]

    pl.when(is_first)(lambda: place_rows(0))
    pl.when(is_second)(lambda: place_rows(RP - ROWS))

    u[:, :, 0:8, :] = jnp.zeros((NCH, 2, 8, CP), F32)
    u[:, :, 104:112, :] = jnp.zeros((NCH, 2, 8, CP), F32)
    for i in range(NCH):
        call[CP * i + CR : CP * (i + 1), :] = jnp.zeros((CP - CR, NCH * CP), BF16)
    total[...] = jnp.zeros_like(total)

    dpad[...] = jnp.zeros_like(dpad)
    dpad[0:LC, 0 : NCH * LC] = dipole[...]
    pads[...] = jnp.full(pads.shape, -1, jnp.int32)
    pads[0:1, 0 : NCH * LC] = target[...].reshape(1, NCH * LC)
    pads[1:2, 0 : NCH * LC] = mom[...].reshape(1, NCH * LC)
    kind = row_iota((64, 1280))
    features = jnp.where(
        kind < 32, (kind == pads[0:1, :]).astype(F32), (kind - 32 == pads[1:2, :]).astype(F32)
    ).astype(BF16)
    row64, col64 = row_iota((64, 64)), lax.broadcasted_iota(jnp.int32, (64, 64), 1)
    m64[...] = jnp.where(jnp.logical_and(row64 >= 32, jnp.abs(row64 - col64) == 1), jnp.where(col64 >= 32, 1.0, 0.0), 0.0)
    m64[0:8, 0:8] = couple_mask[...].astype(F32)
    moments = jnp.where(row_iota((8, 64)) == 0, lax.broadcasted_iota(jnp.int32, (8, 64), 1) - 32, 0)
    moments = jnp.where(lax.broadcasted_iota(jnp.int32, (8, 64), 1) >= 32, moments, 0).astype(F32).astype(BF16)

    def selection(i):
        at = row_iota((512, CP)) + 256 * i - LC * i
        column = lax.broadcasted_iota(jnp.int32, (512, CP), 1)
        return jnp.where(jnp.logical_and(at == column, column < LC), 1.0, 0.0).astype(BF16)

    for i in range(NCH):
        hot[i] = nn_dot(features[:, 256 * i : 256 * i + 512], selection(i))
        lval = nn_dot(moments, hot[i].astype(BF16))[0:1]
        lmom[i : i + 1, :] = lval * (lval + 1.0) * 0.5
    mine = hot[c].T.astype(BF16)
    for i in range(NCH):
        met = nn_dot(mine, nn_dot(m64[...].astype(BF16), hot[i].astype(BF16)).astype(BF16))
        moved = nn_dot(dpad[:, 256 * i : 256 * i + 512], selection(i))
        cloc[:, CP * i : CP * (i + 1)] = jnp.where(met > 1.5, moved, 0.0).astype(BF16)

    call[pl.ds(pl.multiple_of(CP * c, CP), CP), :] = cloc[...]

    def take_matrix(i):
        ham_copy(i).wait()

        def turn(j, _):
            at = pl.ds(pl.multiple_of(128 * j, 128), 128)
            hamt[i, at, :] = stage[i, :, at].T
            return 0

        lax.fori_loop(0, 15, turn, 0)


    greeted = 5 + jnp.where(self_plane, NRAD - 1, 0) + jnp.where(is_root, NRAD - 1, 1)
    pl.semaphore_wait(barrier, greeted)

    def send_term(k, lo, hi):
        ps, slot = lax.rem(k, 2), lax.rem(k, SLOTS)

        @pl.when(k >= 3)
        def _():
            bytes_wait(yrec.at[0, pl.ds(0, 3)], ys_sem.at[ps])

        both = jnp.concatenate([lo, hi], axis=0)
        ysend[ps] = both
        yrec[slot, c] = both
        for d in (2, 1, 3):
            pltpu.make_async_remote_copy(
                src_ref=ysend.at[ps],
                dst_ref=yrec.at[slot, c],
                send_sem=ys_sem.at[ps],
                recv_sem=yr_sem.at[slot],
                device_id=(r, lax.rem(c + d, NCH)),
                device_id_type=MESH,
            ).start()

    def spread(k):
        ps, slot = lax.rem(k, 2), lax.rem(k + SLOTS - 1, SLOTS)

        @pl.when(k >= 3)
        def _():
            bytes_wait(vrec.at[0, pl.ds(0, 31)], vs_sem.at[ps])

        vsend[ps] = term[...].astype(BF16)
        place = vrec.at[slot, 2 * x + core]
        for dz in (2, 1, 3, 0):
            for dx in (2, 1, 3, 0):
                for dc in (1, 0):
                    if dz or dx or dc:
                        rr = 8 * lax.rem(z + dz, 4) + 2 * lax.rem(x + dx, 4) + lax.rem(core + dc, 2)
                        pltpu.make_async_remote_copy(
                            src_ref=vsend.at[ps],
                            dst_ref=place,
                            send_sem=vs_sem.at[ps],
                            recv_sem=vr_sem.at[slot, x],
                            device_id=(rr, c),
                            device_id_type=MESH,
                        ).start()
        pltpu.make_async_copy(vsend.at[ps], place, vr_sem.at[slot, x]).start()

    def send_edge(k, rows):
        slot = lax.rem(k, SLOTS)
        for i in range(4):
            erec[slot, i : i + 1, :] = rows[i]
        for d in range(1, NRAD):
            pltpu.make_async_remote_copy(
                src_ref=erec.at[slot],
                dst_ref=erec.at[slot],
                send_sem=es_sem.at[slot],
                recv_sem=er_sem.at[slot],
                device_id=((d * 11) % NRAD, c),
                device_id_type=MESH,
            ).start()

    def send_strip(k):
        slot = lax.rem(k, SLOTS)
        for s in range(2):
            strec[slot, c, STRIP * s : STRIP * (s + 1), :] = strip[s, 8 : 8 + STRIP, :].astype(BF16)
        for d in (2, 1, 3):
            pltpu.make_async_remote_copy(
                src_ref=strec.at[slot, c],
                dst_ref=strec.at[slot, c],
                send_sem=ss_sem.at[slot],
                recv_sem=sr_sem.at[slot],
                device_id=(0, lax.rem(c + d, NCH)),
                device_id_type=MESH,
            ).start()

    lo, hi = pack(v0p[...])
    term[...] = jnp.concatenate([lo, hi], axis=0)
    itot[...] = term[...]

    @pl.when(is_root)
    def _():
        strip[...] = jnp.zeros_like(strip)
        for s in range(2):
            strip[s, 8 : 8 + STRIP, :] = ut[s, HALO : HALO + STRIP, :]
        stot[...] = jnp.zeros_like(stot)
        send_edge(0, [strip[s, 8 + m : 9 + m, :] for m in range(2) for s in range(2)])
        send_strip(0)

    def halo_copies():
        low = pltpu.make_async_remote_copy(
            src_ref=ut.at[:, pl.ds(HALO, HALO)], dst_ref=ut.at[:, pl.ds(HALO + PTS, HALO)],
            send_sem=hs_sem.at[0], recv_sem=hr_sem.at[0], device_id=(down, c), device_id_type=MESH,
        )
        high = pltpu.make_async_remote_copy(
            src_ref=ut.at[:, pl.ds(PTS, HALO)], dst_ref=ut.at[:, pl.ds(0, HALO)],
            send_sem=hs_sem.at[1], recv_sem=hr_sem.at[1], device_id=(up, c), device_id_type=MESH,
        )
        return low, high

    for cp in halo_copies():
        cp.start()

    def block_copy(d, s):
        cc = lax.rem(c + d, NCH)
        return pltpu.make_async_remote_copy(
            src_ref=ut.at[s, pl.ds(pl.multiple_of(BLK * cc, BLK), BLK + 2 * HALO)],
            dst_ref=u.at[c, s, pl.ds(8, BLK + 2 * HALO)],
            send_sem=us_sem.at[2 * d - 2 + s], recv_sem=ur_sem.at[2 * d - 2 + s],
            device_id=(r, cc), device_id_type=MESH,
        )

    def half(i):
        return pl.ds(pl.multiple_of(CP * i + CR // 2 * core, 32), CR // 2)

    def next_block(p, d):
        return lax.rem(p + (2 if d == 1 else 1), NCH)

    def columns(i):
        return pl.ds(pl.multiple_of(CP * i, CP), CP)

    def coupling_copies(d):
        out = []
        for j in range(2):
            cols = columns(c if j == 0 else next_block(c, d))
            out.append(
                pltpu.make_async_remote_copy(
                    src_ref=cloc.at[half(0), cols],
                    dst_ref=call.at[half(c), cols],
                    send_sem=cs_sem.at[2 * d - 2 + j], recv_sem=cr_sem.at[2 * d - 2 + j],
                    device_id=(r, lax.rem(c + d, NCH)), device_id_type=MESH,
                )
            )
        return out

    def share_copies(d):
        p = lax.rem(c + NCH - d, NCH)
        out = []
        for j in range(2):
            place = call.at[half(p), columns(p if j == 0 else next_block(p, d))]
            out.append(
                pltpu.make_async_remote_copy(
                    src_ref=place, dst_ref=place,
                    send_sem=ds_sem.at[2 * d - 2 + j], recv_sem=dr_sem.at[2 * d - 2 + j],
                    device_id=(r + 1 - 2 * core, c), device_id_type=MESH,
                )
            )
        return out

    def mirror(a, b):
        call[columns(b), columns(a)] = call[columns(a), columns(b)].T

    def final_copy(d):
        cc = lax.rem(c + d, NCH)
        return pltpu.make_async_remote_copy(
            src_ref=total.at[cc], dst_ref=fin.at[c],
            send_sem=fs_sem.at[d - 1], recv_sem=fr_sem.at[d - 1],
            device_id=(r, cc), device_id_type=MESH,
        )

    def own_block():
        return ut[:, pl.ds(pl.multiple_of(BLK * c, BLK), BLK + 2 * HALO), :]

    def outer_step(k):
        f = time_step / lax.convert_element_type(k, F32)
        for cp in range(NCH):
            for s in range(2):
                uh[96 * s : 96 * (s + 1), CP * cp : CP * (cp + 1)] = u[cp, s, 8:104, :].astype(BF16)
        for h in range(2):
            mix[:, 768 * h : 768 * (h + 1)] = nn_dot(uh[...], call[:, 768 * h : 768 * (h + 1)])
        point = PTS * r + BLK * c - HALO + row_iota((96, 1))
        valid = jnp.logical_and(point >= 0, point < NRAD * PTS)
        radius = inner_radius + grid_step * (point.astype(F32) + 1.0)
        inv = 1.0 / (radius * radius)

        def chunk(cc, _):
            applied = []
            for s in range(2):
                w = u[cc, s, 8:104, :]
                lap = (
                    (u[cc, s, 6:102, :] + u[cc, s, 10:106, :])
                    - 16.0 * (u[cc, s, 7:103, :] + u[cc, s, 9:105, :])
                    + 30.0 * w
                )
                applied.append(
                    lap_gain * lap + (lmom[pl.ds(cc, 1), :] * inv) * w + radius * mix[96 * s : 96 * (s + 1), columns(cc)]
                )
            new = (jnp.where(valid, f * applied[1], 0.0), jnp.where(valid, -f * applied[0], 0.0))
            for s in range(2):
                u[cc, s, 8:104, :] = new[s]
                total[cc, s] += new[s][HALO : HALO + BLK]
            return 0

        lax.fori_loop(0, NCH, chunk, 0)

    first = 4

    def outer_when(k, start, index):
        @pl.when(jnp.logical_and(k >= start, k < start + 4))
        def _():
            outer_step(index)

    def step(k, _):
        ps, slot, before = lax.rem(k, 2), lax.rem(k, SLOTS), lax.rem(k + SLOTS - 1, SLOTS)
        f = time_step / lax.convert_element_type(k, F32)

        @pl.when(self_plane)
        def _():
            spread(k)

        rows = jnp.concatenate(unpack(term[0:8], term[8:16]), axis=1).astype(BF16)
        g0, g1 = nt_dot(rows, surf[0]), nt_dot(rows, surf[1])
        ghost = jnp.where(row_iota((8, CP)) < 2, g0, pltpu.roll(g1, 2, 0))[0:4]

        @pl.when(is_root)
        def _():
            grec[slot, 0] = ghost

        @pl.when(jnp.logical_not(is_root))
        def _():
            @pl.when(k >= 3)
            def _():
                bytes_wait(grec.at[0, 0], gs_sem.at[ps])

            gsend[ps] = ghost
            pltpu.make_async_remote_copy(
                src_ref=gsend.at[ps], dst_ref=grec.at[slot, r],
                send_sem=gs_sem.at[ps], recv_sem=gr_sem.at[slot],
                device_id=(0, c), device_id_type=MESH,
            ).start()

        @pl.when(k == 1)
        def _():
            for d in (2, 1, 3):
                for cp in coupling_copies(d):
                    cp.start()
            take_matrix(0)
            take_matrix(1)
            take_matrix(2)

        @pl.when(k == 1)
        def _():
            for cp in halo_copies():
                cp.wait()

            @pl.when(r == NRAD - 1)
            def _():
                ut[:, HALO + PTS :, :] = jnp.zeros((2, HALO, CP), F32)

            u[c, :, 8:104, :] = own_block()
            take_matrix(3)

        @pl.when(k == 2)
        def _():
            for d in (2, 1, 3):
                block_copy(d, 0).start()
            for d in (2, 1, 3):
                for cp in coupling_copies(d):
                    cp.wait()
                for cp in share_copies(d):
                    cp.start()

        @pl.when(k == 3)
        def _():
            for d in (2, 1, 3):
                block_copy(d, 1).start()

        @pl.when(k == first + 4)
        def _():
            for d in (2, 1, 3):
                final_copy(d).start()
            fin[c] = total[c]

        def take_coupling():
            for d in (2, 1, 3):
                for cp in share_copies(d):
                    cp.wait()
            for d in (1, 2, 3):
                mirror(c, lax.rem(c + d, NCH))
                p = lax.rem(c + NCH - d, NCH)
                mirror(p, next_block(p, d))
                block_copy(d, 0).wait()
                block_copy(d, 1).wait()

        outer_when(k, first, 2 * (k - first) + 1)

        acc = jnp.zeros((8, RP), F32)
        for off in (0, 1, 3, 2):
            if off == 2:
                @pl.when(jnp.logical_not(is_root))
                def _():
                    bytes_wait(erec.at[before], er_sem.at[before])

                edge = jnp.concatenate([erec[before], jnp.zeros((4, CP), F32)], axis=0).astype(BF16)
                acc += surface_gain * (nn_dot(edge, surf[0]) + pltpu.roll(nn_dot(edge, surf[1]), 6, 0))

            xi = lax.rem(x + off, 4)
            bytes_wait(vrec.at[before, pl.ds(2 * xi, 2)], vr_sem.at[before, xi])
            tiles = []
            for co in range(2):
                both = vrec[before, 2 * xi + co].astype(F32)
                tiles.append(unpack(both[0:8], both[8:16]))
            lanes = tiles[0][:7] + [tiles[0][7] + tiles[1][0]] + tiles[1][1:]
            lhs = jnp.concatenate(lanes, axis=1).astype(BF16)
            acc += nn_dot(lhs, hamt[xi])

        lo, hi = pack(acc)
        send_term(k, times_minus_i(lo, f), times_minus_i(hi, f))

        @pl.when(is_root)
        def _():
            bytes_wait(strec.at[before, pl.ds(0, 3)], sr_sem.at[before])
            mixed = jnp.zeros((2 * STRIP, CP), F32)
            for cp in range(NCH):
                mixed += nt_dot(strec[before, cp], cloc[:, CP * cp : CP * (cp + 1)])
            bytes_wait(grec.at[slot, pl.ds(0, NRAD - 1)], gr_sem.at[slot])
            seen = jnp.zeros((4, CP), F32)
            for i in range(NRAD):
                seen += grec[slot, i]
            for s in range(2):
                strip[s, 7:8, :] = seen[s : s + 1]
                strip[s, 6:7, :] = seen[2 + s : 3 + s]
            radius = inner_radius + grid_step * (row_iota((STRIP, 1)).astype(F32) + 1.0)
            inv = 1.0 / (radius * radius)
            applied = []
            for s in range(2):
                w = strip[s, 8 : 8 + STRIP, :]
                lap = (
                    (strip[s, 6 : 6 + STRIP, :] + strip[s, 10 : 10 + STRIP, :])
                    - 16.0 * (strip[s, 7 : 7 + STRIP, :] + strip[s, 9 : 9 + STRIP, :])
                    + 30.0 * w
                )
                applied.append(
                    lap_gain * lap + (lmom[pl.ds(c, 1), :] * inv) * w + radius * mixed[STRIP * s : STRIP * (s + 1)]
                )
            new = (f * applied[1], -f * applied[0])
            for s in range(2):
                strip[s, 8 : 8 + STRIP, :] = new[s]
                stot[s] += new[s]
            bytes_wait(strec.at[0, pl.ds(0, 3)], ss_sem.at[before])
            bytes_wait(grec.at[0, pl.ds(0, NRAD - 1)], es_sem.at[before])

            @pl.when(k < ORDER)
            def _():
                send_edge(k, [new[s][m : m + 1] for m in range(2) for s in range(2)])
                send_strip(k)

        pl.when(k == first - 1)(take_coupling)
        outer_when(k, first, 2 * (k - first) + 2)

        bytes_wait(yrec.at[slot, pl.ds(0, 3)], yr_sem.at[slot])
        own = (yrec[slot, 0] + yrec[slot, 1]) + (yrec[slot, 2] + yrec[slot, 3])
        itot[...] += own
        term[...] = own
        return 0

    lax.fori_loop(1, ORDER + 1, step, 0)

    inner = jnp.concatenate(unpack(itot[0:8], itot[8:16]), axis=1)[0:2]

    @pl.when(is_first)
    def _():
        inner_ref[...] = inner[:, 0:ROWS]

    @pl.when(is_second)
    def _():
        inner_ref[...] = inner[:, RP - ROWS : RP]

    for d in (1, 2, 3):
        final_copy(d).wait()

    @pl.when(is_root)
    def _():
        for s in range(2):
            fin[0, s, 0:HALO, :] = stot[s, 0:HALO, :]

    for s in range(2):
        for pb in range(2):
            rows = jnp.concatenate([fin[2 * pb, s], fin[2 * pb + 1, s]], axis=0)
            for cb in range(3):
                n = min(128, LC - 128 * cb)
                out_ref[128 * cb : 128 * cb + n, s, 128 * pb : 128 * (pb + 1)] = (
                    opad[s, 128 * cb : 128 * cb + n, 128 * pb : 128 * (pb + 1)]
                    + rows[:, 128 * cb : 128 * (cb + 1)].T[0:n]
                )

    for k in (ORDER - 1, ORDER):
        bytes_wait(yrec.at[0, pl.ds(0, 3)], ys_sem.at[k % 2])

        @pl.when(self_plane)
        def _():
            bytes_wait(vrec.at[0, pl.ds(0, 31)], vs_sem.at[k % 2])

        @pl.when(jnp.logical_not(is_root))
        def _():
            bytes_wait(grec.at[0, 0], gs_sem.at[k % 2])


def hand_on(out, inner, out_ref, inner_ref):
    out_ref[...] = out[...]
    inner_ref[...] = inner[...]


def local(outer_wave, inner_wave, inner_ham, surface, dipole, ang_mom, target, couple_mask):
    vm = pl.BlockSpec(memory_space=pltpu.VMEM)
    dma = pltpu.SemaphoreType.DMA
    out, inner = pl.pallas_call(
        kernel,
        out_shape=(
            jax.ShapeDtypeStruct((LC, 2, PTS), F32),
            jax.ShapeDtypeStruct((2, ROWS), F32),
        ),
        in_specs=[pl.BlockSpec(memory_space=pl.ANY)] + [vm] * 7,
        out_specs=(vm, vm),
        scratch_shapes=[
            pltpu.VMEM((2, CP, RP), BF16),
            pltpu.VMEM((CP, NCH * CP), BF16),
            pltpu.VMEM((CP, 1280), BF16),
            pltpu.VMEM((8, 1280), jnp.int32),
            pltpu.VMEM((NCH, 64, CP), F32),
            pltpu.VMEM((NCH, CP), F32),
            pltpu.VMEM((64, 64), F32),
            pltpu.VMEM((8, RP), F32),
            pltpu.VMEM((4, RP, 1920), BF16),
            pltpu.VMEM((4, 1920, RP), BF16),
            pltpu.VMEM((2, CP, PTS), F32),
            pltpu.VMEM((2, PTS + 2 * HALO, CP), F32),
            pltpu.VMEM((NCH, 2, 112, CP), F32),
            pltpu.VMEM((192, NCH * CP), BF16),
            pltpu.VMEM((192, NCH * CP), F32),
            pltpu.VMEM((NCH * CP, NCH * CP), BF16),
            pltpu.VMEM((NCH, 2, BLK, CP), F32),
            pltpu.VMEM((NCH, 2, BLK, CP), F32),
            pltpu.VMEM((2, 16, 128), BF16),
            pltpu.VMEM((SLOTS, 32, 16, 128), BF16),
            pltpu.VMEM((2, 16, 128), F32),
            pltpu.VMEM((SLOTS, NCH, 16, 128), F32),
            pltpu.VMEM((16, 128), F32),
            pltpu.VMEM((16, 128), F32),
            pltpu.VMEM((2, 4, CP), F32),
            pltpu.VMEM((SLOTS, NRAD, 4, CP), F32),
            pltpu.VMEM((SLOTS, 4, CP), F32),
            pltpu.VMEM((2, 48, CP), F32),
            pltpu.VMEM((2, STRIP, CP), F32),
            pltpu.VMEM((SLOTS, NCH, 2 * STRIP, CP), BF16),
            dma((4,)),
            dma((2,)), dma((SLOTS, 4)),
            dma((2,)), dma((SLOTS,)),
            dma((2,)), dma((SLOTS,)),
            dma((SLOTS,)), dma((SLOTS,)),
            dma((SLOTS,)), dma((SLOTS,)),
            dma((2,)), dma((2,)),
            dma((6,)), dma((6,)),
            dma((6,)), dma((6,)),
            dma((6,)), dma((6,)),
            dma((3,)), dma((3,)),
        ],
        compiler_params=pltpu.CompilerParams(
            collective_id=0, has_side_effects=True, vmem_limit_bytes=58 * 2**20
        ),
    )(
        inner_ham,
        jnp.transpose(surface, (1, 0, 2)),
        dipole,
        jnp.transpose(outer_wave, (1, 0, 2)),
        inner_wave,
        ang_mom,
        target,
        couple_mask,
    )
    out, inner = pl.pallas_call(
        hand_on,
        out_shape=(jax.ShapeDtypeStruct(out.shape, F32), jax.ShapeDtypeStruct(inner.shape, F32)),
        in_specs=[vm, vm],
        out_specs=(vm, vm),
    )(out, inner)
    return jnp.transpose(out, (1, 0, 2)), inner


def solution(mesh):
    placed = (
        P(None, "chan", "radial"),
        P(None, "radial"),
        P("radial", "chan"),
        P(None, "chan", "radial"),
        P("chan", None),
        P(),
        P(),
        P(),
    )
    return jax.shard_map(
        local,
        mesh=mesh,
        in_specs=placed,
        out_specs=(P(None, "chan", "radial"), P(None, "radial")),
        check_vma=False,
    )
```

```python
import jax
import jax.numpy as jnp
from jax import lax
from jax.experimental import pallas as pl
from jax.experimental.pallas import tpu as pltpu
from jax.sharding import PartitionSpec as P

ORDER = 8
time_step = 0.008
grid_step = 0.08
inner_radius = 20.0
surface_gain = 16.0 / (24.0 * grid_step * grid_step)
lap_gain = 1.0 / (24.0 * grid_step * grid_step)

MESH = pl.DeviceIdType.MESH
F32, BF16 = jnp.float32, jnp.bfloat16
NRAD, NCH = 32, 4
ROWS, LC, PTS = 960, 300, 256
RP, CP = 1024, 384
SLOTS = 4
HALO, BLK = 16, 64
CR = 320
STRIP = 32
NT = (((1,), (1,)), ((), ()))


def nt_dot(a, b):
    return lax.dot_general(a, b, NT, preferred_element_type=F32)


def nn_dot(a, b):
    return jnp.dot(a, b, preferred_element_type=F32)


def bytes_wait(ref, sem):
    pltpu.make_async_copy(ref, ref, sem).wait()


def row_iota(shape):
    return lax.broadcasted_iota(jnp.int32, shape, 0)


def pack(a):
    row = row_iota((8, 128))
    halves = []
    for h in range(2):
        t = a[:, 512 * h : 512 * h + 128]
        for q in range(1, 4):
            piece = a[:, 512 * h + 128 * q : 512 * h + 128 * (q + 1)]
            t = jnp.where(row // 2 == q, pltpu.roll(piece, 2 * q, 0), t)
        halves.append(t)
    return halves


def unpack(lo, hi):
    out = []
    for h in (lo, hi):
        for q in range(4):
            out.append(h if q == 0 else pltpu.roll(h, 8 - 2 * q, 0))
    return out


def times_minus_i(t, f):
    even = row_iota((8, 128)) % 2 == 0
    return jnp.where(even, f * pltpu.roll(t, 7, 0), -f * pltpu.roll(t, 1, 0))


def kernel(
    ham_hbm, surf_in, dipole, outer, v0, mom, target, couple_mask,
    out_ref, inner_ref,
    surf, cloc, dpad, pads, hot, lmom, m64, v0p, stage, hamt, opad, ut, u, uh, mix, call, total, fin,
    vsend, vrec, ysend, yrec, itot, term, gsend, grec, erec, strip, stot, strec,
    ham_sem, vs_sem, vr_sem, ys_sem, yr_sem, gs_sem, gr_sem, es_sem, er_sem, ss_sem, sr_sem,
    hs_sem, hr_sem, us_sem, ur_sem, cs_sem, cr_sem, ds_sem, dr_sem, fs_sem, fr_sem,
):
    r, c = lax.axis_index("radial"), lax.axis_index("chan")
    z, x, core = r // 8, lax.rem(r, 8) // 2, lax.rem(r, 2)
    is_root = r == 0
    self_plane = c == z
    up, down = lax.rem(r + 1, NRAD), lax.rem(r + NRAD - 1, NRAD)

    is_first, is_second = core == 0, core == 1

    zero_rows = jnp.zeros((4, 64, 1920), BF16)
    stage[:, 0:64, :] = zero_rows
    stage[:, ROWS:RP, :] = zero_rows

    def ham_copy(i):
        return pltpu.make_async_copy(
            ham_hbm.at[:, pl.ds(1920 * i, 1920)],
            stage.at[i, pl.ds(pl.multiple_of(64 * core, 64), ROWS)],
            ham_sem.at[i],
        )

    for i in range(4):
        ham_copy(i).start()

    barrier = pltpu.get_barrier_semaphore()

    def greet(device):
        pl.semaphore_signal(barrier, inc=1, device_id=device, device_id_type=MESH)

    for i in range(8):
        producer = 8 * c + i

        @pl.when(producer != r)
        def _():
            greet((producer, c))

    for d in range(1, NCH):
        greet((r, lax.rem(c + d, NCH)))
    greet((up, c))
    greet((down, c))

    @pl.when(is_root)
    def _():
        for d in range(1, NRAD):
            greet((d, c))

    @pl.when(jnp.logical_not(is_root))
    def _():
        greet((0, c))

    opad[:, 256:CP, :] = jnp.zeros((2, CP - 256, PTS), F32)
    for s in range(2):
        opad[s, 0:LC, :] = outer[:, s, :]
    for s in range(2):
        for cb in range(3):
            for pb in range(2):
                ut[s, HALO + 128 * pb : HALO + 128 * (pb + 1), 128 * cb : 128 * (cb + 1)] = opad[
                    s, 128 * cb : 128 * (cb + 1), 128 * pb : 128 * (pb + 1)
                ].T
    surf[...] = jnp.zeros_like(surf)
    v0p[...] = jnp.zeros_like(v0p)

    def place_rows(at):
        for m in range(2):
            surf[m, 0:LC, at : at + ROWS] = surf_in[:, m, :]
        v0p[0:2, at : at + ROWS] = v0[...]

    pl.when(is_first)(lambda: place_rows(0))
    pl.when(is_second)(lambda: place_rows(RP - ROWS))

    u[:, :, 0:8, :] = jnp.zeros((NCH, 2, 8, CP), F32)
    u[:, :, 104:112, :] = jnp.zeros((NCH, 2, 8, CP), F32)
    for i in range(NCH):
        call[CP * i + CR : CP * (i + 1), :] = jnp.zeros((CP - CR, NCH * CP), BF16)
    total[...] = jnp.zeros_like(total)

    dpad[...] = jnp.zeros_like(dpad)
    dpad[0:LC, 0 : NCH * LC] = dipole[...]
    pads[...] = jnp.full(pads.shape, -1, jnp.int32)
    pads[0:1, 0 : NCH * LC] = target[...].reshape(1, NCH * LC)
    pads[1:2, 0 : NCH * LC] = mom[...].reshape(1, NCH * LC)
    kind = row_iota((64, 1280))
    features = jnp.where(
        kind < 32, (kind == pads[0:1, :]).astype(F32), (kind - 32 == pads[1:2, :]).astype(F32)
    ).astype(BF16)
    row64, col64 = row_iota((64, 64)), lax.broadcasted_iota(jnp.int32, (64, 64), 1)
    m64[...] = jnp.where(jnp.logical_and(row64 >= 32, jnp.abs(row64 - col64) == 1), jnp.where(col64 >= 32, 1.0, 0.0), 0.0)
    m64[0:8, 0:8] = couple_mask[...].astype(F32)
    moments = jnp.where(row_iota((8, 64)) == 0, lax.broadcasted_iota(jnp.int32, (8, 64), 1) - 32, 0)
    moments = jnp.where(lax.broadcasted_iota(jnp.int32, (8, 64), 1) >= 32, moments, 0).astype(F32).astype(BF16)

    def selection(i):
        at = row_iota((512, CP)) + 256 * i - LC * i
        column = lax.broadcasted_iota(jnp.int32, (512, CP), 1)
        return jnp.where(jnp.logical_and(at == column, column < LC), 1.0, 0.0).astype(BF16)

    for i in range(NCH):
        hot[i] = nn_dot(features[:, 256 * i : 256 * i + 512], selection(i))
        lval = nn_dot(moments, hot[i].astype(BF16))[0:1]
        lmom[i : i + 1, :] = lval * (lval + 1.0) * 0.5
    mine = hot[c].T.astype(BF16)
    for i in range(NCH):
        met = nn_dot(mine, nn_dot(m64[...].astype(BF16), hot[i].astype(BF16)).astype(BF16))
        moved = nn_dot(dpad[:, 256 * i : 256 * i + 512], selection(i))
        cloc[:, CP * i : CP * (i + 1)] = jnp.where(met > 1.5, moved, 0.0).astype(BF16)

    call[pl.ds(pl.multiple_of(CP * c, CP), CP), :] = cloc[...]

    def take_matrix(i):
        ham_copy(i).wait()

        def turn(j, _):
            at = pl.ds(pl.multiple_of(128 * j, 128), 128)
            hamt[i, at, :] = stage[i, :, at].T
            return 0

        lax.fori_loop(0, 15, turn, 0)


    greeted = 5 + jnp.where(self_plane, NRAD - 1, 0) + jnp.where(is_root, NRAD - 1, 1)
    pl.semaphore_wait(barrier, greeted)

    def send_term(k, lo, hi):
        ps, slot = lax.rem(k, 2), lax.rem(k, SLOTS)

        @pl.when(k >= 3)
        def _():
            bytes_wait(yrec.at[0, pl.ds(0, 3)], ys_sem.at[ps])

        both = jnp.concatenate([lo, hi], axis=0)
        ysend[ps] = both
        yrec[slot, c] = both
        for d in (2, 1, 3):
            pltpu.make_async_remote_copy(
                src_ref=ysend.at[ps],
                dst_ref=yrec.at[slot, c],
                send_sem=ys_sem.at[ps],
                recv_sem=yr_sem.at[slot],
                device_id=(r, lax.rem(c + d, NCH)),
                device_id_type=MESH,
            ).start()

    def spread(k):
        ps, slot = lax.rem(k, 2), lax.rem(k + SLOTS - 1, SLOTS)

        @pl.when(k >= 3)
        def _():
            bytes_wait(vrec.at[0, pl.ds(0, 31)], vs_sem.at[ps])

        vsend[ps] = term[...].astype(BF16)
        place = vrec.at[slot, 2 * x + core]
        for dz in (2, 1, 3, 0):
            for dx in (2, 1, 3, 0):
                for dc in (1, 0):
                    if dz or dx or dc:
                        rr = 8 * lax.rem(z + dz, 4) + 2 * lax.rem(x + dx, 4) + lax.rem(core + dc, 2)
                        pltpu.make_async_remote_copy(
                            src_ref=vsend.at[ps],
                            dst_ref=place,
                            send_sem=vs_sem.at[ps],
                            recv_sem=vr_sem.at[slot, x],
                            device_id=(rr, c),
                            device_id_type=MESH,
                        ).start()
        pltpu.make_async_copy(vsend.at[ps], place, vr_sem.at[slot, x]).start()

    def send_edge(k, rows):
        slot = lax.rem(k, SLOTS)
        for i in range(4):
            erec[slot, i : i + 1, :] = rows[i]
        for d in range(1, NRAD):
            pltpu.make_async_remote_copy(
                src_ref=erec.at[slot],
                dst_ref=erec.at[slot],
                send_sem=es_sem.at[slot],
                recv_sem=er_sem.at[slot],
                device_id=((d * 11) % NRAD, c),
                device_id_type=MESH,
            ).start()

    def send_strip(k):
        slot = lax.rem(k, SLOTS)
        for s in range(2):
            strec[slot, c, STRIP * s : STRIP * (s + 1), :] = strip[s, 8 : 8 + STRIP, :].astype(BF16)
        for d in (2, 1, 3):
            pltpu.make_async_remote_copy(
                src_ref=strec.at[slot, c],
                dst_ref=strec.at[slot, c],
                send_sem=ss_sem.at[slot],
                recv_sem=sr_sem.at[slot],
                device_id=(0, lax.rem(c + d, NCH)),
                device_id_type=MESH,
            ).start()

    lo, hi = pack(v0p[...])
    term[...] = jnp.concatenate([lo, hi], axis=0)
    itot[...] = term[...]

    @pl.when(is_root)
    def _():
        strip[...] = jnp.zeros_like(strip)
        for s in range(2):
            strip[s, 8 : 8 + STRIP, :] = ut[s, HALO : HALO + STRIP, :]
        stot[...] = jnp.zeros_like(stot)
        send_edge(0, [strip[s, 8 + m : 9 + m, :] for m in range(2) for s in range(2)])
        send_strip(0)

    def halo_copies():
        low = pltpu.make_async_remote_copy(
            src_ref=ut.at[:, pl.ds(HALO, HALO)], dst_ref=ut.at[:, pl.ds(HALO + PTS, HALO)],
            send_sem=hs_sem.at[0], recv_sem=hr_sem.at[0], device_id=(down, c), device_id_type=MESH,
        )
        high = pltpu.make_async_remote_copy(
            src_ref=ut.at[:, pl.ds(PTS, HALO)], dst_ref=ut.at[:, pl.ds(0, HALO)],
            send_sem=hs_sem.at[1], recv_sem=hr_sem.at[1], device_id=(up, c), device_id_type=MESH,
        )
        return low, high

    for cp in halo_copies():
        cp.start()

    def block_copy(d, s):
        cc = lax.rem(c + d, NCH)
        return pltpu.make_async_remote_copy(
            src_ref=ut.at[s, pl.ds(pl.multiple_of(BLK * cc, BLK), BLK + 2 * HALO)],
            dst_ref=u.at[c, s, pl.ds(8, BLK + 2 * HALO)],
            send_sem=us_sem.at[2 * d - 2 + s], recv_sem=ur_sem.at[2 * d - 2 + s],
            device_id=(r, cc), device_id_type=MESH,
        )

    def half(i):
        return pl.ds(pl.multiple_of(CP * i + CR // 2 * core, 32), CR // 2)

    def next_block(p, d):
        return lax.rem(p + (2 if d == 1 else 1), NCH)

    def columns(i):
        return pl.ds(pl.multiple_of(CP * i, CP), CP)

    def coupling_copies(d):
        out = []
        for j in range(2):
            cols = columns(c if j == 0 else next_block(c, d))
            out.append(
                pltpu.make_async_remote_copy(
                    src_ref=cloc.at[half(0), cols],
                    dst_ref=call.at[half(c), cols],
                    send_sem=cs_sem.at[2 * d - 2 + j], recv_sem=cr_sem.at[2 * d - 2 + j],
                    device_id=(r, lax.rem(c + d, NCH)), device_id_type=MESH,
                )
            )
        return out

    def share_copies(d):
        p = lax.rem(c + NCH - d, NCH)
        out = []
        for j in range(2):
            place = call.at[half(p), columns(p if j == 0 else next_block(p, d))]
            out.append(
                pltpu.make_async_remote_copy(
                    src_ref=place, dst_ref=place,
                    send_sem=ds_sem.at[2 * d - 2 + j], recv_sem=dr_sem.at[2 * d - 2 + j],
                    device_id=(r + 1 - 2 * core, c), device_id_type=MESH,
                )
            )
        return out

    def mirror(a, b):
        call[columns(b), columns(a)] = call[columns(a), columns(b)].T

    def final_copy(d, s):
        cc = lax.rem(c + d, NCH)
        return pltpu.make_async_remote_copy(
            src_ref=total.at[cc, s], dst_ref=fin.at[c, s],
            send_sem=fs_sem.at[2 * d - 2 + s], recv_sem=fr_sem.at[2 * d - 2 + s],
            device_id=(r, cc), device_id_type=MESH,
        )

    def own_block():
        return ut[:, pl.ds(pl.multiple_of(BLK * c, BLK), BLK + 2 * HALO), :]

    def outer_step(k):
        f = time_step / lax.convert_element_type(k, F32)
        for cp in range(NCH):
            for s in range(2):
                uh[96 * s : 96 * (s + 1), CP * cp : CP * (cp + 1)] = u[cp, s, 8:104, :].astype(BF16)
        for h in range(2):
            mix[:, 768 * h : 768 * (h + 1)] = nn_dot(uh[...], call[:, 768 * h : 768 * (h + 1)])
        point = PTS * r + BLK * c - HALO + row_iota((96, 1))
        valid = jnp.logical_and(point >= 0, point < NRAD * PTS)
        radius = inner_radius + grid_step * (point.astype(F32) + 1.0)
        inv = 1.0 / (radius * radius)

        def chunk(cc, _):
            applied = []
            for s in range(2):
                w = u[cc, s, 8:104, :]
                lap = (
                    (u[cc, s, 6:102, :] + u[cc, s, 10:106, :])
                    - 16.0 * (u[cc, s, 7:103, :] + u[cc, s, 9:105, :])
                    + 30.0 * w
                )
                applied.append(
                    lap_gain * lap + (lmom[pl.ds(cc, 1), :] * inv) * w + radius * mix[96 * s : 96 * (s + 1), columns(cc)]
                )
            new = (jnp.where(valid, f * applied[1], 0.0), jnp.where(valid, -f * applied[0], 0.0))
            for s in range(2):
                u[cc, s, 8:104, :] = new[s]
                total[cc, s] += new[s][HALO : HALO + BLK]
            return 0

        lax.fori_loop(0, NCH, chunk, 0)

    first = 4

    def outer_when(k, start, index):
        @pl.when(jnp.logical_and(k >= start, k < start + 4))
        def _():
            outer_step(index)

    def step(k, _):
        ps, slot, before = lax.rem(k, 2), lax.rem(k, SLOTS), lax.rem(k + SLOTS - 1, SLOTS)
        f = time_step / lax.convert_element_type(k, F32)

        @pl.when(self_plane)
        def _():
            spread(k)

        rows = jnp.concatenate(unpack(term[0:8], term[8:16]), axis=1).astype(BF16)
        g0, g1 = nt_dot(rows, surf[0]), nt_dot(rows, surf[1])
        ghost = jnp.where(row_iota((8, CP)) < 2, g0, pltpu.roll(g1, 2, 0))[0:4]

        @pl.when(is_root)
        def _():
            grec[slot, 0] = ghost

        @pl.when(jnp.logical_not(is_root))
        def _():
            @pl.when(k >= 3)
            def _():
                bytes_wait(grec.at[0, 0], gs_sem.at[ps])

            gsend[ps] = ghost
            pltpu.make_async_remote_copy(
                src_ref=gsend.at[ps], dst_ref=grec.at[slot, r],
                send_sem=gs_sem.at[ps], recv_sem=gr_sem.at[slot],
                device_id=(0, c), device_id_type=MESH,
            ).start()

        @pl.when(k == 1)
        def _():
            for d in (2, 1, 3):
                for cp in coupling_copies(d):
                    cp.start()
            take_matrix(0)
            take_matrix(1)
            take_matrix(2)

        @pl.when(k == 1)
        def _():
            for cp in halo_copies():
                cp.wait()

            @pl.when(r == NRAD - 1)
            def _():
                ut[:, HALO + PTS :, :] = jnp.zeros((2, HALO, CP), F32)

            u[c, :, 8:104, :] = own_block()
            take_matrix(3)

        @pl.when(k == 2)
        def _():
            for d in (2, 1, 3):
                block_copy(d, 0).start()
            for d in (2, 1, 3):
                for cp in coupling_copies(d):
                    cp.wait()
                for cp in share_copies(d):
                    cp.start()

        @pl.when(k == 3)
        def _():
            for d in (2, 1, 3):
                block_copy(d, 1).start()

        @pl.when(k == first + 4)
        def _():
            for d in (2, 1, 3):
                final_copy(d, 1).start()
            fin[c] = total[c]

        def take_coupling():
            for d in (2, 1, 3):
                for cp in share_copies(d):
                    cp.wait()
            for d in (1, 2, 3):
                mirror(c, lax.rem(c + d, NCH))
                p = lax.rem(c + NCH - d, NCH)
                mirror(p, next_block(p, d))
                block_copy(d, 0).wait()
                block_copy(d, 1).wait()

        outer_when(k, first, 2 * (k - first) + 1)

        acc = jnp.zeros((8, RP), F32)
        for off in (0, 1, 3, 2):
            if off == 2:
                @pl.when(jnp.logical_not(is_root))
                def _():
                    bytes_wait(erec.at[before], er_sem.at[before])

                edge = jnp.concatenate([erec[before], jnp.zeros((4, CP), F32)], axis=0).astype(BF16)
                acc += surface_gain * (nn_dot(edge, surf[0]) + pltpu.roll(nn_dot(edge, surf[1]), 6, 0))

            xi = lax.rem(x + off, 4)
            bytes_wait(vrec.at[before, pl.ds(2 * xi, 2)], vr_sem.at[before, xi])
            tiles = []
            for co in range(2):
                both = vrec[before, 2 * xi + co].astype(F32)
                tiles.append(unpack(both[0:8], both[8:16]))
            lanes = tiles[0][:7] + [tiles[0][7] + tiles[1][0]] + tiles[1][1:]
            lhs = jnp.concatenate(lanes, axis=1).astype(BF16)
            acc += nn_dot(lhs, hamt[xi])

        lo, hi = pack(acc)
        send_term(k, times_minus_i(lo, f), times_minus_i(hi, f))

        @pl.when(is_root)
        def _():
            bytes_wait(strec.at[before, pl.ds(0, 3)], sr_sem.at[before])
            mixed = jnp.zeros((2 * STRIP, CP), F32)
            for cp in range(NCH):
                mixed += nt_dot(strec[before, cp], cloc[:, CP * cp : CP * (cp + 1)])
            bytes_wait(grec.at[slot, pl.ds(0, NRAD - 1)], gr_sem.at[slot])
            seen = jnp.zeros((4, CP), F32)
            for i in range(NRAD):
                seen += grec[slot, i]
            for s in range(2):
                strip[s, 7:8, :] = seen[s : s + 1]
                strip[s, 6:7, :] = seen[2 + s : 3 + s]
            radius = inner_radius + grid_step * (row_iota((STRIP, 1)).astype(F32) + 1.0)
            inv = 1.0 / (radius * radius)
            applied = []
            for s in range(2):
                w = strip[s, 8 : 8 + STRIP, :]
                lap = (
                    (strip[s, 6 : 6 + STRIP, :] + strip[s, 10 : 10 + STRIP, :])
                    - 16.0 * (strip[s, 7 : 7 + STRIP, :] + strip[s, 9 : 9 + STRIP, :])
                    + 30.0 * w
                )
                applied.append(
                    lap_gain * lap + (lmom[pl.ds(c, 1), :] * inv) * w + radius * mixed[STRIP * s : STRIP * (s + 1)]
                )
            new = (f * applied[1], -f * applied[0])
            for s in range(2):
                strip[s, 8 : 8 + STRIP, :] = new[s]
                stot[s] += new[s]
            bytes_wait(strec.at[0, pl.ds(0, 3)], ss_sem.at[before])
            bytes_wait(grec.at[0, pl.ds(0, NRAD - 1)], es_sem.at[before])

            @pl.when(k < ORDER)
            def _():
                send_edge(k, [new[s][m : m + 1] for m in range(2) for s in range(2)])
                send_strip(k)

        pl.when(k == first - 1)(take_coupling)
        outer_when(k, first, 2 * (k - first) + 2)

        @pl.when(k == first + 3)
        def _():
            for d in (2, 1, 3):
                final_copy(d, 0).start()

        bytes_wait(yrec.at[slot, pl.ds(0, 3)], yr_sem.at[slot])
        own = (yrec[slot, 0] + yrec[slot, 1]) + (yrec[slot, 2] + yrec[slot, 3])
        itot[...] += own
        term[...] = own
        return 0

    lax.fori_loop(1, ORDER + 1, step, 0)

    inner = jnp.concatenate(unpack(itot[0:8], itot[8:16]), axis=1)[0:2]

    @pl.when(is_first)
    def _():
        inner_ref[...] = inner[:, 0:ROWS]

    @pl.when(is_second)
    def _():
        inner_ref[...] = inner[:, RP - ROWS : RP]

    for d in (1, 2, 3):
        final_copy(d, 0).wait()
        final_copy(d, 1).wait()

    @pl.when(is_root)
    def _():
        for s in range(2):
            fin[0, s, 0:HALO, :] = stot[s, 0:HALO, :]

    for s in range(2):
        for pb in range(2):
            rows = jnp.concatenate([fin[2 * pb, s], fin[2 * pb + 1, s]], axis=0)
            for cb in range(3):
                n = min(128, LC - 128 * cb)
                out_ref[128 * cb : 128 * cb + n, s, 128 * pb : 128 * (pb + 1)] = (
                    opad[s, 128 * cb : 128 * cb + n, 128 * pb : 128 * (pb + 1)]
                    + rows[:, 128 * cb : 128 * (cb + 1)].T[0:n]
                )

    for k in (ORDER - 1, ORDER):
        bytes_wait(yrec.at[0, pl.ds(0, 3)], ys_sem.at[k % 2])

        @pl.when(self_plane)
        def _():
            bytes_wait(vrec.at[0, pl.ds(0, 31)], vs_sem.at[k % 2])

        @pl.when(jnp.logical_not(is_root))
        def _():
            bytes_wait(grec.at[0, 0], gs_sem.at[k % 2])


def hand_on(out, inner, out_ref, inner_ref):
    out_ref[...] = out[...]
    inner_ref[...] = inner[...]


def local(outer_wave, inner_wave, inner_ham, surface, dipole, ang_mom, target, couple_mask):
    vm = pl.BlockSpec(memory_space=pltpu.VMEM)
    dma = pltpu.SemaphoreType.DMA
    out, inner = pl.pallas_call(
        kernel,
        out_shape=(
            jax.ShapeDtypeStruct((LC, 2, PTS), F32),
            jax.ShapeDtypeStruct((2, ROWS), F32),
        ),
        in_specs=[pl.BlockSpec(memory_space=pl.ANY)] + [vm] * 7,
        out_specs=(vm, vm),
        scratch_shapes=[
            pltpu.VMEM((2, CP, RP), BF16),
            pltpu.VMEM((CP, NCH * CP), BF16),
            pltpu.VMEM((CP, 1280), BF16),
            pltpu.VMEM((8, 1280), jnp.int32),
            pltpu.VMEM((NCH, 64, CP), F32),
            pltpu.VMEM((NCH, CP), F32),
            pltpu.VMEM((64, 64), F32),
            pltpu.VMEM((8, RP), F32),
            pltpu.VMEM((4, RP, 1920), BF16),
            pltpu.VMEM((4, 1920, RP), BF16),
            pltpu.VMEM((2, CP, PTS), F32),
            pltpu.VMEM((2, PTS + 2 * HALO, CP), F32),
            pltpu.VMEM((NCH, 2, 112, CP), F32),
            pltpu.VMEM((192, NCH * CP), BF16),
            pltpu.VMEM((192, NCH * CP), F32),
            pltpu.VMEM((NCH * CP, NCH * CP), BF16),
            pltpu.VMEM((NCH, 2, BLK, CP), F32),
            pltpu.VMEM((NCH, 2, BLK, CP), F32),
            pltpu.VMEM((2, 16, 128), BF16),
            pltpu.VMEM((SLOTS, 32, 16, 128), BF16),
            pltpu.VMEM((2, 16, 128), F32),
            pltpu.VMEM((SLOTS, NCH, 16, 128), F32),
            pltpu.VMEM((16, 128), F32),
            pltpu.VMEM((16, 128), F32),
            pltpu.VMEM((2, 4, CP), F32),
            pltpu.VMEM((SLOTS, NRAD, 4, CP), F32),
            pltpu.VMEM((SLOTS, 4, CP), F32),
            pltpu.VMEM((2, 48, CP), F32),
            pltpu.VMEM((2, STRIP, CP), F32),
            pltpu.VMEM((SLOTS, NCH, 2 * STRIP, CP), BF16),
            dma((4,)),
            dma((2,)), dma((SLOTS, 4)),
            dma((2,)), dma((SLOTS,)),
            dma((2,)), dma((SLOTS,)),
            dma((SLOTS,)), dma((SLOTS,)),
            dma((SLOTS,)), dma((SLOTS,)),
            dma((2,)), dma((2,)),
            dma((6,)), dma((6,)),
            dma((6,)), dma((6,)),
            dma((6,)), dma((6,)),
            dma((6,)), dma((6,)),
        ],
        compiler_params=pltpu.CompilerParams(
            collective_id=0, has_side_effects=True, vmem_limit_bytes=58 * 2**20
        ),
    )(
        inner_ham,
        jnp.transpose(surface, (1, 0, 2)),
        dipole,
        jnp.transpose(outer_wave, (1, 0, 2)),
        inner_wave,
        ang_mom,
        target,
        couple_mask,
    )
    out, inner = pl.pallas_call(
        hand_on,
        out_shape=(jax.ShapeDtypeStruct(out.shape, F32), jax.ShapeDtypeStruct(inner.shape, F32)),
        in_specs=[vm, vm],
        out_specs=(vm, vm),
    )(out, inner)
    return jnp.transpose(out, (1, 0, 2)), inner


def solution(mesh):
    placed = (
        P(None, "chan", "radial"),
        P(None, "radial"),
        P("radial", "chan"),
        P(None, "chan", "radial"),
        P("chan", None),
        P(),
        P(),
        P(),
    )
    return jax.shard_map(
        local,
        mesh=mesh,
        in_specs=placed,
        out_specs=(P(None, "chan", "radial"), P(None, "radial")),
        check_vma=False,
    )
```
